128 devices in a mesh: sec: 16 (over z, x), freq: 8 (over y, core).
Axes of the slice: x: 4, y: 4, z: 4, core: 2. Of those that a mesh axis runs over, the one named last changes fastest.
Arguments:
- coupling: float32 [128, 28800], P('sec'), may hold values from -1 to 1
- propagation: float32 [128, 120], P('sec'), may hold values from 0.5 to 3
- frequency_offset: float32 [64], P('freq'), may hold values from -3.140625 to 3.140625
- measured: float32 [64, 28800], P('freq'), may hold values from -0.54 to 0.54
Outputs:
- gradients: float32 [128, 28800], P('sec')
The draws below stay inside these ranges and needn't reach their ends.
All inputs are finite; a program needn't handle non-finite values.
Results may differ from the reference program's by a relative error of at most 0.0003.
Values sent between devices are 32-bit elements; how exact they have to be, the bound alone decides.
No kernel may reach another device: no remote copies, remote signals or barrier semaphores. Data moves between devices by JAX's collectives and lax.ppermute only.
A program may use at most 128 MiB of HBM per device.

```python
import jax
import jax.numpy as jnp
from jax import lax

M = 120
K_DEV = 8
K = 128
F = 64
N_SEC = 16


highest = lax.Precision.HIGHEST


def complex_pair_product(left_real, left_imag, right_real, right_imag):
    real_part = jnp.einsum('kij,kjl->kil', left_real, right_real, precision=highest) - jnp.einsum('kij,kjl->kil', left_imag, right_imag, precision=highest)
    imag_part = jnp.einsum('kij,kjl->kil', left_real, right_imag, precision=highest) + jnp.einsum('kij,kjl->kil', left_imag, right_real, precision=highest)
    return (real_part, imag_part)


def draw_coupling(key, part):
    key = jax.random.fold_in(key, 11)
    key_real, key_imag, key_loss = jax.random.split(key, 3)
    extent = (K, M, M)
    spread = 0.6
    real_part = jax.random.truncated_normal(key_real, -4.0, 4.0, extent, jnp.float32)
    imag_part = jax.random.truncated_normal(key_imag, -4.0, 4.0, extent, jnp.float32)
    scaling = spread / jnp.sqrt(2.0 * M)
    unit = jnp.eye(M, dtype=jnp.float32)[None]
    current_real = (unit + scaling * real_part) / 1.6
    current_imag = scaling * imag_part / 1.6
    for sweep in range(16):
        gram_real, gram_imag = complex_pair_product(jnp.swapaxes(current_real, -1, -2), -jnp.swapaxes(current_imag, -1, -2), current_real, current_imag)
        factor_real = 1.5 * unit - 0.5 * gram_real
        factor_imag = -0.5 * gram_imag
        current_real, current_imag = complex_pair_product(current_real, current_imag, factor_real, factor_imag)
    loss = jnp.exp(0.02 * jax.random.uniform(key_loss, (K, M, 1), jnp.float32, -1.0, 0.0))
    whole = jnp.concatenate([current_real * loss, current_imag * loss], axis=-1)
    whole = jnp.clip(whole, -1.0, 1.0)
    return whole.reshape(K, 2 * M * M)


def levels(rng, shape, pieces, least, top_value):
    level, own = 1.0, jax.random.fold_in(rng, 6)
    for dim, shards_of in pieces:
        steps = jnp.exp(jax.random.uniform(jax.random.fold_in(own, dim), (shards_of,), jnp.float32, least / len(pieces), top_value / len(pieces)))
        level = level * jnp.repeat(steps, shape[dim] // shards_of).reshape([-1 if axis == dim else 1 for axis in range(len(shape))])
    return level


def bell_draw(own_key, shape, deviation, most, cuts=(), held_as=jnp.bfloat16):
    array = jax.random.normal(own_key, shape, jnp.float32) * deviation
    if len(cuts) > 0:
        array = levels(own_key, shape, cuts, -0.22, 0.18) * array
    return jnp.clip(array, min=-most, max=most).astype(held_as)


def setup_inputs(seed: int = 0) -> dict:
    splits = jax.random.split(jax.random.key(seed), 5)
    return {
        "coupling": draw_coupling(jax.random.fold_in(splits[4], 71), 0),
        "propagation": jnp.clip(0.5 + 2.5 * jax.random.uniform(splits[1], (K, M), jnp.float32) ** levels(splits[1], (K, M), ((0, 16),), -0.2, 0.2), 0.5, 3.0),
        "frequency_offset": jnp.clip(jax.random.uniform(splits[2], (F,), jnp.float32, -3.140625, 3.140625), -3.140625, 3.140625),
        "measured": bell_draw(splits[3], (F, 2 * M * M), 0.09, 0.54, ((0, 8),), jnp.float32),
    }


highest = lax.Precision.HIGHEST


def complex_product(outer_matrix, inner_matrix):
    mode_count = outer_matrix.shape[-2]
    from_real = jnp.einsum('...ij,...jk->...ik', outer_matrix[..., :mode_count], inner_matrix, precision=highest)
    from_imag = jnp.einsum('...ij,...jk->...ik', outer_matrix[..., mode_count:], inner_matrix, precision=highest)
    return jnp.concatenate([from_real[..., :mode_count] - from_imag[..., mode_count:], from_real[..., mode_count:] + from_imag[..., :mode_count]], axis=-1)


def adjoint(matrix):
    mode_count = matrix.shape[-2]
    real_part = jnp.swapaxes(matrix[..., :mode_count], -1, -2)
    imag_part = jnp.swapaxes(matrix[..., mode_count:], -1, -2)
    return jnp.concatenate([real_part, -imag_part], axis=-1)


def rotate_rows(matrix, phases):
    mode_count = matrix.shape[-2]
    cosine_rows = jnp.cos(phases)[..., None]
    sine_rows = jnp.sin(phases)[..., None]
    real_part = matrix[..., :mode_count]
    imag_part = matrix[..., mode_count:]
    return jnp.concatenate([cosine_rows * real_part - sine_rows * imag_part, cosine_rows * imag_part + sine_rows * real_part], axis=-1)


def identity_stack(freq_count, mode_count):
    unit = jnp.broadcast_to(jnp.eye(mode_count, dtype=jnp.float32), (freq_count, mode_count, mode_count))
    return jnp.concatenate([unit, jnp.zeros_like(unit)], axis=-1)


def frequency_term(pulled, before):
    mode_count = pulled.shape[-2]
    swapped = jnp.concatenate([pulled[..., mode_count:], -pulled[..., :mode_count]], axis=-1)
    real_part = jnp.einsum('fij,flj->il', pulled, before, precision=highest)
    imag_part = jnp.einsum('fij,flj->il', swapped, before, precision=highest)
    return 2.0 * jnp.concatenate([real_part, imag_part], axis=-1)


def reference(coupling, propagation, frequency_offset, measured):
    mode_count = propagation.shape[1]
    freq_count = frequency_offset.shape[0]
    coupling = coupling.reshape(-1, mode_count, 2 * mode_count)
    measured = measured.reshape(-1, mode_count, 2 * mode_count)
    identity = identity_stack(freq_count, mode_count)
    block_coupling = coupling.reshape(N_SEC, K_DEV, mode_count, 2 * mode_count)
    block_phase = propagation.reshape(N_SEC, K_DEV, mode_count)

    def advance(prefix, inputs):
        section_coupling, section_phase = inputs
        phases = frequency_offset[:, None] * section_phase[None, :]
        product = complex_product(rotate_rows(section_coupling[None], phases), prefix)
        return product, prefix

    def block_step(prefix, inputs):
        product, _ = lax.scan(advance, prefix, inputs)
        return product, prefix

    total_map, starts = lax.scan(block_step, identity, (block_coupling, block_phase))
    misfit = total_map - measured

    def back_block(adjoint_state, inputs):
        couplings, phase_rows, start = inputs
        _, befores = lax.scan(advance, start, (couplings, phase_rows))

        def retreat(back_state, items):
            section_coupling, section_phase, before = items
            phases = frequency_offset[:, None] * section_phase[None, :]
            pulled = rotate_rows(back_state, -phases)
            gradient = frequency_term(pulled, before)
            return complex_product(adjoint(section_coupling)[None], pulled), gradient

        return lax.scan(retreat, adjoint_state, (couplings, phase_rows, befores), reverse=True)

    _, gradients = lax.scan(back_block, misfit, (block_coupling, block_phase, starts), reverse=True)
    return gradients.reshape(N_SEC * K_DEV, 2 * mode_count * mode_count)
```

```python
import functools

import jax
import jax.numpy as jnp
from jax import lax
from jax.experimental import pallas as pl
from jax.experimental.pallas import tpu as pltpu
from jax.sharding import Mesh, PartitionSpec as P

M = 120
W = 2 * M
L = 128
ND = 8
F32, BF16 = jnp.float32, jnp.bfloat16
PARAMS = pltpu.CompilerParams(vmem_limit_bytes=56 * 1024 * 1024)
VMEM = pl.BlockSpec(memory_space=pltpu.VMEM)
SMEM = pl.BlockSpec(memory_space=pltpu.SMEM)


def shape(*dims):
    return jax.ShapeDtypeStruct(dims, F32)


def split(x):
    high = x.astype(BF16)
    return high, (x - high.astype(F32)).astype(BF16)


def right_form(x):
    real, imag = x[:, :L], x[:, L:]
    return jnp.concatenate([x, jnp.concatenate([-imag, real], axis=1)], axis=0)


def dot(a, b):
    return jnp.dot(a, b, preferred_element_type=F32)


def product(left, right):
    left_high, left_low = split(left)
    right_high, right_low = split(right_form(right))
    return dot(left_high, right_high) + (dot(left_low, right_high) + dot(left_high, right_low))


def scaled(x, cosine, sine):
    real, imag = x[:, :L], x[:, L:]
    return jnp.concatenate([cosine * real - sine * imag, cosine * imag + sine * real], axis=1)


def adjoint(x):
    return jnp.concatenate([x[:, :L].T, -x[:, L:].T], axis=1)


def padded(x):
    return jnp.concatenate([x, jnp.zeros((L - M, 2 * L), F32)], axis=0)


def unpack_rows(flat_ref, out_ref):
    out_ref[...] = jnp.zeros(out_ref.shape, F32)
    zeros = jnp.zeros((ND, L - M), F32)
    for m in range(M):
        rows = pl.ds(m, ND, stride=L)
        real = flat_ref[:, m * W : m * W + M]
        imag = flat_ref[:, m * W + M : (m + 1) * W]
        out_ref[0, rows, :] = jnp.concatenate([real, zeros], axis=1)
        out_ref[1, rows, :] = jnp.concatenate([imag, zeros], axis=1)


def unpacked(rows_ref, start):
    return jnp.concatenate([rows_ref[0, pl.ds(start, L), :], rows_ref[1, pl.ds(start, L), :]], axis=1)


def up_kernel(freq_ref, prop_ref, flat_ref, a_ref, c_ref, tab_ref, tabt_ref, p_ref, q_ref, lhs_ref):
    tab_ref[...] = jnp.zeros(tab_ref.shape, F32)
    for f in range(ND):
        phase = prop_ref[...] * freq_ref[f]
        tab_ref[0, f * ND : (f + 1) * ND, 0:M] = jnp.cos(phase)
        tab_ref[1, f * ND : (f + 1) * ND, 0:M] = jnp.sin(phase)
    tabt_ref[0] = tab_ref[0].T
    tabt_ref[1] = tab_ref[1].T
    unpack_rows(flat_ref, c_ref)

    def columns(x, k, f):
        i = f * ND + k
        return scaled(x, tab_ref[0, i : i + 1, :], tab_ref[1, i : i + 1, :])

    def rows(x, k, f):
        i = f * ND + k
        return scaled(x, tabt_ref[0, :, i : i + 1], tabt_ref[1, :, i : i + 1])

    for j in range(4):
        low, up = 2 * j, 2 * j + 1
        c_up = unpacked(c_ref, up * L)
        for f in range(ND):
            lhs_ref[f * L : (f + 1) * L, :] = columns(c_up, low, f)
        res = product(lhs_ref[...], unpacked(c_ref, low * L))
        for f in range(ND):
            one = res[f * L : (f + 1) * L]
            p_ref[j, f] = rows(one, up, f) if j % 2 == 0 else one
    for f in range(ND):
        q0 = rows(product(p_ref[1, f], p_ref[0, f]), 3, f)
        q1 = product(p_ref[3, f], p_ref[2, f])
        q_ref[0, f] = q0
        q_ref[1, f] = q1
        a_ref[f] = rows(product(q1, q0), 7, f)[:M]


def up(freq, prop, flat):
    return pl.pallas_call(
        up_kernel,
        out_shape=(
            shape(ND, M, 2 * L),
            shape(2, ND * L, L),
            shape(2, ND * ND, L),
            shape(2, L, ND * ND),
            shape(4, ND, L, 2 * L),
            shape(2, ND, L, 2 * L),
        ),
        in_specs=[SMEM, VMEM, VMEM],
        out_specs=(VMEM,) * 6,
        scratch_shapes=[pltpu.VMEM((ND * L, 2 * L), F32)],
        compiler_params=PARAMS,
        name="up",
    )(freq, prop, flat)


def half_kernel(r_ref, flat_ref, h_ref, m_ref, p_ref, q_ref, rows_ref):
    for j in range(4):
        p_ref[j] = product(padded(r_ref[2 * j + 1]), padded(r_ref[2 * j]))
    for j in range(2):
        q_ref[j] = product(p_ref[2 * j + 1], p_ref[2 * j])
    h_ref[...] = product(q_ref[1], q_ref[0])[:M]
    unpack_rows(flat_ref, rows_ref)
    own = (lax.axis_index("zl") * 4 + lax.axis_index("x") + 4 * lax.axis_index("zh")) % ND
    m_ref[...] = unpacked(rows_ref, pl.multiple_of(own * L, L))


def half(r, flat):
    return pl.pallas_call(
        half_kernel,
        out_shape=(shape(M, 2 * L), shape(L, 2 * L), shape(4, L, 2 * L), shape(2, L, 2 * L)),
        in_specs=[VMEM, VMEM],
        out_specs=(VMEM,) * 4,
        scratch_shapes=[pltpu.VMEM((2, ND * L, L), F32)],
        compiler_params=PARAMS,
        name="half",
    )(r, flat)


def top_kernel(r_ref, m_ref, p_ref, q_ref, h_ref, other_ref, v_ref):
    upper = lax.axis_index("zh") == 1
    own, other = padded(h_ref[...]), padded(other_ref[...])
    h0 = jnp.where(upper, other, own)
    h1 = jnp.where(upper, own, other)
    misfit = adjoint(product(h1, h0) - m_ref[...])
    v = product(jnp.where(upper, h0, misfit), jnp.where(upper, misfit, h1))
    v0, v1 = product(v, q_ref[1]), product(q_ref[0], v)
    pairs = (product(v0, p_ref[1]), product(p_ref[0], v0), product(v1, p_ref[3]), product(p_ref[2], v1))
    for j in range(4):
        v_ref[2 * j] = product(pairs[j], padded(r_ref[2 * j + 1]))[:M]
        v_ref[2 * j + 1] = product(padded(r_ref[2 * j]), pairs[j])[:M]


def top(r, m, p, q, h, other):
    return pl.pallas_call(
        top_kernel,
        out_shape=shape(ND, M, 2 * L),
        in_specs=[VMEM] * 6,
        out_specs=VMEM,
        compiler_params=PARAMS,
        name="top",
    )(r, m, p, q, h, other)


def down_kernel(v_ref, c_ref, tab_ref, tabt_ref, p_ref, q_ref, g_ref, vp_ref):
    def columns(x, k, f):
        i = f * ND + k
        return scaled(x, tab_ref[0, i : i + 1, :], tab_ref[1, i : i + 1, :])

    def rows(x, k, f):
        i = f * ND + k
        return scaled(x, tabt_ref[0, :, i : i + 1], tabt_ref[1, :, i : i + 1])

    for f in range(ND):
        v = columns(padded(v_ref[f]), 7, f)
        v0 = columns(product(v, q_ref[1, f]), 3, f)
        v1 = product(q_ref[0, f], v)
        at = pl.ds(f * L, L)
        vp_ref[0, at] = columns(product(v0, p_ref[1, f]), 1, f)
        vp_ref[1, at] = product(p_ref[0, f], v0)
        vp_ref[2, at] = columns(product(v1, p_ref[3, f]), 5, f)
        vp_ref[3, at] = product(p_ref[2, f], v1)

    core, y = lax.axis_index("c"), lax.axis_index("y")

    def place(k):
        return jnp.where(core == k // 4, 0, 4) + (k % 4 - y + 4) % 4

    for j in range(4):
        low, up = 2 * j, 2 * j + 1
        c_low = unpacked(c_ref, low * L)
        res = product(vp_ref[j], unpacked(c_ref, up * L))
        g_low = columns(res[0:L], low, 0)
        g_up = rows(product(c_low, vp_ref[j, 0:L]), low, 0)
        for f in range(1, ND):
            g_low += columns(res[f * L : (f + 1) * L], low, f)
            g_up += rows(product(c_low, vp_ref[j, f * L : (f + 1) * L]), low, f)
        g_ref[place(low)] = g_low[:M]
        g_ref[place(up)] = g_up[:M]


def down(v, c, tab, tabt, p, q):
    return pl.pallas_call(
        down_kernel,
        out_shape=shape(ND, M, 2 * L),
        in_specs=[VMEM] * 6,
        out_specs=VMEM,
        scratch_shapes=[pltpu.VMEM((4, ND * L, 2 * L), F32)],
        compiler_params=PARAMS,
        name="down",
    )(v, c, tab, tabt, p, q)


def sum_kernel(own_ref, a_ref, b_ref, c_ref, out_ref):
    total = (own_ref[...] + a_ref[...]) + (b_ref[...] + c_ref[...])
    out_ref[...] = 2.0 * adjoint(padded(total))[:M]


def sum_up(own, a, b, c):
    return pl.pallas_call(
        sum_kernel,
        out_shape=shape(M, 2 * L),
        in_specs=[VMEM] * 4,
        out_specs=VMEM,
        compiler_params=PARAMS,
        name="sum_up",
    )(own, a, b, c)


def store_kernel(*refs):
    parts, out_ref, rows_ref = refs[:ND], refs[ND], refs[ND + 1]
    core, y = lax.axis_index("c"), lax.axis_index("y")
    for i in range(ND):
        place = (4 * core if i < 4 else 4 * (1 - core)) + (y - i % 4 + 4) % 4
        at = pl.ds(pl.multiple_of(place * L, L), M)
        rows_ref[0, at, :] = parts[i][:, :L]
        rows_ref[1, at, :] = parts[i][:, L:]
    for m in range(M):
        rows = pl.ds(m, ND, stride=L)
        out_ref[:, m * W : m * W + M] = rows_ref[0, rows, :][:, :M]
        out_ref[:, m * W + M : (m + 1) * W] = rows_ref[1, rows, :][:, :M]


def store(parts):
    return pl.pallas_call(
        store_kernel,
        out_shape=shape(ND, M * W),
        in_specs=[VMEM] * ND,
        out_specs=VMEM,
        scratch_shapes=[pltpu.VMEM((2, ND * L, L), F32)],
        compiler_params=PARAMS,
        name="store",
    )(*parts)


def shards(coupling, propagation, frequency_offset, measured):
    upper = lax.axis_index("zh") == 1
    freq = jnp.where(upper, jnp.roll(frequency_offset, 4), frequency_offset)
    a, c, tab, tabt, p, q = up(freq, propagation, coupling)
    r = lax.all_to_all(a, ("zl", "x"), 0, 0, tiled=True)
    h, m, hp, hq = half(r, measured)
    other = lax.ppermute(h, ("zh", "zl"), [(0, 3), (1, 2), (2, 1), (3, 0)])
    v = top(r, m, hp, hq, h, other)
    v = lax.all_to_all(v, ("zl", "x"), 0, 0, tiled=True)
    g = down(v, c, tab, tabt, p, q)
    swap = [(0, 1), (1, 0)]
    g = g[:4] + lax.ppermute(g[4:], "c", swap)
    turned = lambda i, x: lax.ppermute(x, "y", [(s, (s + i) % 4) for s in range(4)])
    total = sum_up(g[0], *[turned(i, g[i]) for i in range(1, 4)])
    parts = [total] + [turned(i, total) for i in range(1, 4)]
    parts += [lax.ppermute(x, "c", swap) for x in parts]
    return store(parts)


def solution(mesh):
    fine = Mesh(mesh.devices.reshape(2, 2, 4, 4, 2), ("zh", "zl", "x", "y", "c"))
    sec, freq = ("zh", "zl", "x"), ("y", "c")
    return jax.shard_map(
        shards,
        mesh=fine,
        in_specs=(P(sec, None), P(sec, None), P(freq), P(freq, None)),
        out_specs=P(sec, None),
        check_vma=False,
    )
```

```python
import functools

import jax
import jax.numpy as jnp
from jax import lax
from jax.experimental import pallas as pl
from jax.experimental.pallas import tpu as pltpu
from jax.sharding import Mesh, PartitionSpec as P

M = 120
W = 2 * M
L = 128
ND = 8
F32, BF16 = jnp.float32, jnp.bfloat16
PARAMS = pltpu.CompilerParams(vmem_limit_bytes=20 * 1024 * 1024)
VMEM = pl.BlockSpec(memory_space=pltpu.VMEM)
SMEM = pl.BlockSpec(memory_space=pltpu.SMEM)


def shape(*dims):
    return jax.ShapeDtypeStruct(dims, F32)


def split(x):
    high = x.astype(BF16)
    return high, (x - high.astype(F32)).astype(BF16)


def right_form(x):
    real, imag = x[:, :L], x[:, L:]
    return jnp.concatenate([x, jnp.concatenate([-imag, real], axis=1)], axis=0)


def dot(a, b):
    return jnp.dot(a, b, preferred_element_type=F32)


def product(left, right):
    left_high, left_low = split(left)
    right_high, right_low = split(right_form(right))
    return dot(left_high, right_high) + (dot(left_low, right_high) + dot(left_high, right_low))


def scaled(x, cosine, sine):
    real, imag = x[:, :L], x[:, L:]
    return jnp.concatenate([cosine * real - sine * imag, cosine * imag + sine * real], axis=1)


def adjoint(x):
    return jnp.concatenate([x[:, :L].T, -x[:, L:].T], axis=1)


def padded(x):
    return jnp.concatenate([x, jnp.zeros((L - M, 2 * L), F32)], axis=0)


def unpack_rows(flat_ref, out_ref):
    out_ref[...] = jnp.zeros(out_ref.shape, F32)
    zeros = jnp.zeros((ND, L - M), F32)
    for m in range(M):
        rows = pl.ds(m, ND, stride=L)
        real = flat_ref[:, m * W : m * W + M]
        imag = flat_ref[:, m * W + M : (m + 1) * W]
        out_ref[0, rows, :] = jnp.concatenate([real, zeros], axis=1)
        out_ref[1, rows, :] = jnp.concatenate([imag, zeros], axis=1)


def unpacked(rows_ref, start):
    return jnp.concatenate([rows_ref[0, pl.ds(start, L), :], rows_ref[1, pl.ds(start, L), :]], axis=1)


OFFSETS = (6, 2, 7, 5, 4, 3, 1, 0)
HALF = ND // 2


def number():
    return lax.axis_index("zl") * 4 + lax.axis_index("x")


def owned():
    return number() ^ (lax.axis_index("zh") * 4)


def scalings(tab_ref, tabt_ref):
    def columns(x, k, f):
        i = f * ND + k
        return scaled(x, tab_ref[0, i : i + 1, :], tab_ref[1, i : i + 1, :])

    def rows(x, k, f):
        i = f * ND + k
        return scaled(x, tabt_ref[0, :, i : i + 1], tabt_ref[1, :, i : i + 1])

    return columns, rows


def up_half(first, a_refs, c_ref, tab_ref, tabt_ref, p_ref, q_ref, lhs_ref):
    columns, rows = scalings(tab_ref, tabt_ref)
    for j in range(4):
        low, up = 2 * j, 2 * j + 1
        c_up = unpacked(c_ref, up * L)
        for f in range(HALF):
            lhs_ref[f * L : (f + 1) * L, :] = columns(c_up, low, first + f)
        res = product(lhs_ref[...], unpacked(c_ref, low * L))
        for f in range(HALF):
            one = res[f * L : (f + 1) * L]
            p_ref[j, f] = rows(one, up, first + f) if j % 2 == 0 else one
    for f in range(HALF):
        q0 = rows(product(p_ref[1, f], p_ref[0, f]), 3, first + f)
        q1 = product(p_ref[3, f], p_ref[2, f])
        q_ref[0, f] = q0
        q_ref[1, f] = q1
        a_refs[f][...] = rows(product(q1, q0), 7, first + f)[:M]


def up_first_kernel(freq_ref, prop_ref, flat_ref, c_ref, tab_ref, tabt_ref, p_ref, q_ref, *refs):
    tab_ref[...] = jnp.zeros(tab_ref.shape, F32)
    for f in range(ND):
        phase = prop_ref[...] * freq_ref[owned() ^ OFFSETS[f]]
        tab_ref[0, f * ND : (f + 1) * ND, 0:M] = jnp.cos(phase)
        tab_ref[1, f * ND : (f + 1) * ND, 0:M] = jnp.sin(phase)
    tabt_ref[0] = tab_ref[0].T
    tabt_ref[1] = tab_ref[1].T
    unpack_rows(flat_ref, c_ref)
    up_half(0, refs[:HALF], c_ref, tab_ref, tabt_ref, p_ref, q_ref, refs[HALF])


def up_second_kernel(c_ref, tab_ref, tabt_ref, p_ref, q_ref, *refs):
    up_half(HALF, refs[:HALF], c_ref, tab_ref, tabt_ref, p_ref, q_ref, refs[HALF])


NODES = (shape(4, HALF, L, 2 * L), shape(2, HALF, L, 2 * L))
LHS = [pltpu.VMEM((HALF * L, 2 * L), F32)]


def up_first(freq, prop, flat):
    tables = (shape(2, ND * L, L), shape(2, ND * ND, L), shape(2, L, ND * ND))
    outs = tables + NODES + (shape(M, 2 * L),) * HALF
    res = pl.pallas_call(
        up_first_kernel,
        out_shape=outs,
        in_specs=[SMEM, VMEM, VMEM],
        out_specs=(VMEM,) * len(outs),
        scratch_shapes=LHS,
        compiler_params=PARAMS,
        name="up_first",
    )(freq, prop, flat)
    return res[:3], res[3:5], res[5:]


def up_second(tables):
    outs = NODES + (shape(M, 2 * L),) * HALF
    res = pl.pallas_call(
        up_second_kernel,
        out_shape=outs,
        in_specs=[VMEM] * 3,
        out_specs=(VMEM,) * len(outs),
        scratch_shapes=LHS,
        compiler_params=PARAMS,
        name="up_second",
    )(*tables)
    return res[:2], res[2:]


def half_kernel(*refs):
    received, (h_ref, r_ref, p_ref, q_ref) = refs[:ND], refs[ND:]
    me = number()
    for i, offset in enumerate(OFFSETS):
        r_ref[me ^ offset] = padded(received[i][...])
    for j in range(4):
        p_ref[j] = product(r_ref[2 * j + 1], r_ref[2 * j])
    for j in range(2):
        q_ref[j] = product(p_ref[2 * j + 1], p_ref[2 * j])
    h_ref[...] = product(q_ref[1], q_ref[0])[:M]


def half(received):
    return pl.pallas_call(
        half_kernel,
        out_shape=(shape(M, 2 * L), shape(ND, L, 2 * L), shape(4, L, 2 * L), shape(2, L, 2 * L)),
        in_specs=[VMEM] * ND,
        out_specs=(VMEM,) * 4,
        compiler_params=PARAMS,
        name="half",
    )(*received)


def pick_kernel(flat_ref, m_ref, rows_ref):
    unpack_rows(flat_ref, rows_ref)
    m_ref[...] = unpacked(rows_ref, pl.multiple_of(owned() * L, L))


def pick(flat):
    return pl.pallas_call(
        pick_kernel,
        out_shape=shape(L, 2 * L),
        in_specs=[VMEM],
        out_specs=VMEM,
        scratch_shapes=[pltpu.VMEM((2, ND * L, L), F32)],
        compiler_params=PARAMS,
        name="pick",
    )(flat)


def top_kernel(r_ref, m_ref, p_ref, q_ref, h_ref, other_ref, *refs):
    v_refs, leaf_ref = refs[:ND], refs[ND]
    upper = lax.axis_index("zh") == 1
    own, other = padded(h_ref[...]), padded(other_ref[...])
    h0 = jnp.where(upper, other, own)
    h1 = jnp.where(upper, own, other)
    misfit = adjoint(product(h1, h0) - m_ref[...])
    v = product(jnp.where(upper, h0, misfit), jnp.where(upper, misfit, h1))
    v0, v1 = product(v, q_ref[1]), product(q_ref[0], v)
    pairs = (product(v0, p_ref[1]), product(p_ref[0], v0), product(v1, p_ref[3]), product(p_ref[2], v1))
    for j in range(4):
        leaf_ref[2 * j] = product(pairs[j], r_ref[2 * j + 1])[:M]
        leaf_ref[2 * j + 1] = product(r_ref[2 * j], pairs[j])[:M]
    me = number()
    for i, offset in enumerate(OFFSETS):
        v_refs[i][...] = leaf_ref[me ^ offset]


def top(r, m, p, q, h, other):
    return pl.pallas_call(
        top_kernel,
        out_shape=(shape(M, 2 * L),) * ND,
        in_specs=[VMEM] * 6,
        out_specs=(VMEM,) * ND,
        scratch_shapes=[pltpu.VMEM((ND, M, 2 * L), F32)],
        compiler_params=PARAMS,
        name="top",
    )(r, m, p, q, h, other)


def quad_down(quad, first, v, c_ref, tab_ref, tabt_ref, p_ref, q_ref, vp_ref):
    columns, rows = scalings(tab_ref, tabt_ref)
    for f in range(HALF):
        if quad == 0:
            mine = columns(product(v[f], q_ref[1, f]), 3, first + f)
        else:
            mine = product(q_ref[0, f], v[f])
        at = pl.ds(f * L, L)
        vp_ref[0, at] = columns(product(mine, p_ref[2 * quad + 1, f]), 4 * quad + 1, first + f)
        vp_ref[1, at] = product(p_ref[2 * quad, f], mine)
    out = []
    for j in range(2):
        low, up = 4 * quad + 2 * j, 4 * quad + 2 * j + 1
        c_low = unpacked(c_ref, low * L)
        res = product(vp_ref[j], unpacked(c_ref, up * L))
        g_low = columns(res[0:L], low, first)
        g_up = rows(product(c_low, vp_ref[j, 0:L]), low, first)
        for f in range(1, HALF):
            g_low += columns(res[f * L : (f + 1) * L], low, first + f)
            g_up += rows(product(c_low, vp_ref[j, f * L : (f + 1) * L]), low, first + f)
        out += [g_low[:M], g_up[:M]]
    return out


def whole_v(first, v_refs, tab_ref, tabt_ref):
    columns, _ = scalings(tab_ref, tabt_ref)
    return [columns(padded(v_refs[f][...]), 7, first + f) for f in range(HALF)]


def down_first_kernel(*refs):
    v_refs, (c_ref, tab_ref, tabt_ref, p_ref, q_ref, g_ref, vp_ref) = refs[:HALF], refs[HALF:]
    v = whole_v(0, v_refs, tab_ref, tabt_ref)
    for quad in range(2):
        res = quad_down(quad, 0, v, c_ref, tab_ref, tabt_ref, p_ref, q_ref, vp_ref)
        for i in range(4):
            g_ref[4 * quad + i] = res[i]


VP = [pltpu.VMEM((2, HALF * L, 2 * L), F32)]


def down_first(v, tables, nodes):
    return pl.pallas_call(
        down_first_kernel,
        out_shape=shape(ND, M, 2 * L),
        in_specs=[VMEM] * (HALF + 5),
        out_specs=VMEM,
        scratch_shapes=VP,
        compiler_params=PARAMS,
        name="down_first",
    )(*v, *tables, *nodes)


def down_second_kernel(mine, *refs):
    v_refs, (c_ref, tab_ref, tabt_ref, p_ref, q_ref, part_ref, g_ref, vp_ref) = refs[:HALF], refs[HALF:]
    core, y = lax.axis_index("c"), lax.axis_index("y")
    for quad in range(2):

        @pl.when(core == (quad if mine else 1 - quad))
        def _():
            v = whole_v(HALF, v_refs, tab_ref, tabt_ref)
            res = quad_down(quad, HALF, v, c_ref, tab_ref, tabt_ref, p_ref, q_ref, vp_ref)
            for i in range(4):
                g_ref[(i - y + 4) % 4] = res[i] + part_ref[4 * quad + i]


def down_second(mine, v, tables, nodes, part):
    return pl.pallas_call(
        functools.partial(down_second_kernel, mine),
        out_shape=shape(4, M, 2 * L),
        in_specs=[VMEM] * (HALF + 6),
        out_specs=VMEM,
        scratch_shapes=VP,
        compiler_params=PARAMS,
        name="down_mine" if mine else "down_theirs",
    )(*v, *tables, *nodes, part)


def sum_kernel(own_ref, a_ref, b_ref, c_ref, out_ref):
    total = (own_ref[...] + a_ref[...]) + (b_ref[...] + c_ref[...])
    out_ref[...] = 2.0 * adjoint(padded(total))[:M]


def sum_up(own, a, b, c):
    return pl.pallas_call(
        sum_kernel,
        out_shape=shape(M, 2 * L),
        in_specs=[VMEM] * 4,
        out_specs=VMEM,
        compiler_params=PARAMS,
        name="sum_up",
    )(own, a, b, c)


def store_kernel(*refs):
    parts, out_ref, rows_ref = refs[:ND], refs[ND], refs[ND + 1]
    core, y = lax.axis_index("c"), lax.axis_index("y")
    for i in range(ND):
        place = (4 * core if i < 4 else 4 * (1 - core)) + (y - i % 4 + 4) % 4
        at = pl.ds(pl.multiple_of(place * L, L), M)
        rows_ref[0, at, :] = parts[i][:, :L]
        rows_ref[1, at, :] = parts[i][:, L:]
    for m in range(M):
        rows = pl.ds(m, ND, stride=L)
        out_ref[:, m * W : m * W + M] = rows_ref[0, rows, :][:, :M]
        out_ref[:, m * W + M : (m + 1) * W] = rows_ref[1, rows, :][:, :M]


def store(parts):
    return pl.pallas_call(
        store_kernel,
        out_shape=shape(ND, M * W),
        in_specs=[VMEM] * ND,
        out_specs=VMEM,
        scratch_shapes=[pltpu.VMEM((2, ND * L, L), F32)],
        compiler_params=PARAMS,
        name="store",
    )(*parts)


def shards(coupling, propagation, frequency_offset, measured):
    swap = [(0, 1), (1, 0)]

    def exchange(offset, x):
        return lax.ppermute(x, ("zl", "x"), [(s, s ^ offset) for s in range(ND)]) if offset else x

    def turned(i, x):
        return lax.ppermute(x, "y", [(s, (s + i) % 4) for s in range(4)])

    tables, nodes_first, a_first = up_first(frequency_offset, propagation, coupling)
    nodes_second, a_second = up_second(tables)
    received = [exchange(offset, a) for offset, a in zip(OFFSETS, (*a_first, *a_second))]
    h, r, p, q = half(received)
    other = lax.ppermute(h, ("zh", "zl"), [(0, 3), (1, 2), (2, 1), (3, 0)])
    v = top(r, pick(measured), p, q, h, other)
    v = [exchange(offset, x) for offset, x in zip(OFFSETS, v)]
    part = down_first(v[:HALF], tables, nodes_first)
    theirs = down_second(False, v[HALF:], tables, nodes_second, part)
    received = lax.ppermute(theirs, "c", swap)
    mine = down_second(True, v[HALF:], tables, nodes_second, part)
    g = mine + received
    total = sum_up(g[0], *[turned(i, g[i]) for i in range(1, 4)])
    parts = [total] + [turned(i, total) for i in range(1, 4)]
    parts += [lax.ppermute(x, "c", swap) for x in parts]
    return store(parts)


def solution(mesh):
    fine = Mesh(mesh.devices.reshape(2, 2, 4, 4, 2), ("zh", "zl", "x", "y", "c"))
    sec, freq = ("zh", "zl", "x"), ("y", "c")
    return jax.shard_map(
        shards,
        mesh=fine,
        in_specs=(P(sec, None), P(sec, None), P(freq), P(freq, None)),
        out_specs=P(sec, None),
        check_vma=False,
    )
```

```python
import functools

import jax
import jax.numpy as jnp
from jax import lax
from jax.experimental import pallas as pl
from jax.experimental.pallas import tpu as pltpu
from jax.sharding import Mesh, PartitionSpec as P

M = 120
W = 2 * M
L = 128
ND = 8
F32, BF16 = jnp.float32, jnp.bfloat16
PARAMS = pltpu.CompilerParams(vmem_limit_bytes=20 * 1024 * 1024)
VMEM = pl.BlockSpec(memory_space=pltpu.VMEM)
SMEM = pl.BlockSpec(memory_space=pltpu.SMEM)
HBM = pl.BlockSpec(memory_space=pltpu.HBM)

OFFSETS = (6, 2, 7, 5, 4, 3, 1, 0)
UP_GROUPS = ((0, 1, 2), (3, 4, 5, 6, 7))
DOWN_GROUPS = ((7, 0, 1), (2, 3, 4, 5, 6))
NODES = 2 * len(UP_GROUPS)
ROWS = ((0, 32), (32, 64), (64, 96), (96, 120))


def single(*dims):
    return jax.ShapeDtypeStruct(dims, F32)


def halves(*dims):
    return jax.ShapeDtypeStruct((*dims, 2, L, 2 * L), BF16)


def split(x):
    high = x.astype(BF16)
    return high, (x - high.astype(F32)).astype(BF16)


def right_form(x):
    real, imag = x[:, :L], x[:, L:]
    return jnp.concatenate([x, jnp.concatenate([-imag, real], axis=1)], axis=0)


def product(left, right):
    (left_high, left_low), (right_high, right_low) = left, right
    right_high, right_low = right_form(right_high), right_form(right_low)
    return jnp.dot(
        jnp.concatenate([left_high, left_low, left_high], axis=1),
        jnp.concatenate([right_high, right_high, right_low], axis=0),
        preferred_element_type=F32,
    )


def load(ref, *at):
    return ref[(*at, 0)], ref[(*at, 1)]


def keep(ref, x, *at):
    ref[(*at, 0)], ref[(*at, 1)] = split(x)


def scaled(x, cosine, sine):
    real, imag = x[:, :L], x[:, L:]
    return jnp.concatenate([cosine * real - sine * imag, cosine * imag + sine * real], axis=1)


def adjoint(x):
    return jnp.concatenate([x[:, :L].T, -x[:, L:].T], axis=1)


def padded(x):
    return jnp.concatenate([x, jnp.zeros((L - M, 2 * L), F32)], axis=0)


def start_rows(flat_ref, buffer_ref, sems):
    copies = []
    for i, (a, b) in enumerate(ROWS):
        at = (slice(None), pl.ds(a * W, (b - a) * W))
        copies.append(pltpu.make_async_copy(flat_ref.at[at], buffer_ref.at[at], sems.at[i]))
        copies[-1].start()
    return copies


def unpack_rows(copies, buffer_ref, out_ref):
    zeros = jnp.zeros((ND, L - M), F32)
    for (a, b), copy in zip(ROWS, copies):
        copy.wait()
        for m in range(a, b):
            rows = pl.ds(m, ND, stride=L)
            real = buffer_ref[:, m * W : m * W + M]
            imag = buffer_ref[:, m * W + M : (m + 1) * W]
            out_ref[0, rows, :] = jnp.concatenate([real, zeros], axis=1)
            out_ref[1, rows, :] = jnp.concatenate([imag, zeros], axis=1)
    for k in range(ND):
        out_ref[:, k * L + M : (k + 1) * L, :] = jnp.zeros((2, L - M, L), F32)


def unpacked(rows_ref, start):
    return jnp.concatenate([rows_ref[0, pl.ds(start, L), :], rows_ref[1, pl.ds(start, L), :]], axis=1)


ROW_SCRATCH = [pltpu.VMEM((ND, M * W), F32), pltpu.SemaphoreType.DMA((len(ROWS),))]


def number():
    return lax.axis_index("zl") * 4 + lax.axis_index("x")


def owned():
    return number() ^ (lax.axis_index("zh") * 4)


def scalings(tab_ref, tabt_ref):
    def columns(x, k, f):
        i = f * ND + k
        return scaled(x, tab_ref[0, i : i + 1, :], tab_ref[1, i : i + 1, :])

    def rows(x, k, f):
        i = f * ND + k
        return scaled(x, tabt_ref[0, :, i : i + 1], tabt_ref[1, :, i : i + 1])

    return columns, rows


def up_group(group, a_refs, c_ref, ch_ref, tab_ref, tabt_ref, p_ref, q_ref, lhs_ref):
    columns, rows = scalings(tab_ref, tabt_ref)
    count = len(group)
    for j in range(4):
        low, up = 2 * j, 2 * j + 1
        c_up = unpacked(c_ref, up * L)
        for i, f in enumerate(group):
            at = slice(i * L, (i + 1) * L)
            lhs_ref[j, 0, at], lhs_ref[j, 1, at] = split(columns(c_up, low, f))
        res = product(load(lhs_ref, j), load(ch_ref, low))
        for i, f in enumerate(group):
            one = res[i * L : (i + 1) * L]
            keep(p_ref, rows(one, up, f) if j % 2 == 0 else one, j, i)
    for i, f in enumerate(group):
        keep(q_ref, rows(product(load(p_ref, 1, i), load(p_ref, 0, i)), 3, f), 0, i)
    for i, f in enumerate(group):
        keep(q_ref, product(load(p_ref, 3, i), load(p_ref, 2, i)), 1, i)
    for i, f in enumerate(group):
        a_refs[i][...] = rows(product(load(q_ref, 1, i), load(q_ref, 0, i)), 7, f)[:M]


def up_kernel(group, freq_hbm, prop_hbm, flat_hbm, c_ref, ch_ref, tab_ref, tabt_ref, p_ref, q_ref, *refs):
    count = len(group)
    a_refs, (lhs_ref, freq_ref, prop_ref, small, buffer_ref, sems) = refs[:count], refs[count:]
    first = pltpu.make_async_copy(freq_hbm, freq_ref, small.at[0])
    second = pltpu.make_async_copy(prop_hbm, prop_ref, small.at[1])
    first.start()
    second.start()
    copies = start_rows(flat_hbm, buffer_ref, sems)
    tab_ref[...] = jnp.zeros(tab_ref.shape, F32)
    first.wait()
    second.wait()
    for f in range(ND):
        phase = prop_ref[...] * freq_ref[owned() ^ OFFSETS[f]]
        tab_ref[0, f * ND : (f + 1) * ND, 0:M] = jnp.cos(phase)
        tab_ref[1, f * ND : (f + 1) * ND, 0:M] = jnp.sin(phase)
    tabt_ref[0] = tab_ref[0].T
    tabt_ref[1] = tab_ref[1].T
    unpack_rows(copies, buffer_ref, c_ref)
    for k in range(ND):
        keep(ch_ref, unpacked(c_ref, k * L), k)
    up_group(group, a_refs, c_ref, ch_ref, tab_ref, tabt_ref, p_ref, q_ref, lhs_ref)


def up_second_kernel(group, c_ref, ch_ref, tab_ref, tabt_ref, p_ref, q_ref, *refs):
    a_refs, (lhs_ref,) = refs[: len(group)], refs[len(group) :]
    up_group(group, a_refs, c_ref, ch_ref, tab_ref, tabt_ref, p_ref, q_ref, lhs_ref)


def up_outs(group):
    count = len(group)
    return (halves(4, count), halves(2, count)) + (single(M, 2 * L),) * count


def lhs_scratch(group):
    return pltpu.VMEM((4, 2, len(group) * L, 2 * L), BF16)


def in_hbm(x):
    return pltpu.with_memory_space_constraint(x, pltpu.HBM)


def up(group, freq, prop, flat):
    tables = (single(2, ND * L, L), halves(ND), single(2, ND * ND, L), single(2, L, ND * ND))
    outs = tables + up_outs(group)
    res = pl.pallas_call(
        functools.partial(up_kernel, group),
        out_shape=outs,
        in_specs=[HBM, HBM, HBM],
        out_specs=(VMEM,) * len(outs),
        scratch_shapes=[
            lhs_scratch(group),
            pltpu.SMEM((ND,), F32),
            pltpu.VMEM((ND, M), F32),
            pltpu.SemaphoreType.DMA((2,)),
            *ROW_SCRATCH,
        ],
        compiler_params=PARAMS,
        name="up",
    )(in_hbm(freq), in_hbm(prop), in_hbm(flat))
    return res[:4], res[4:6], res[6:]


def up_second(group, tables):
    outs = up_outs(group)
    res = pl.pallas_call(
        functools.partial(up_second_kernel, group),
        out_shape=outs,
        in_specs=[VMEM] * 4,
        out_specs=(VMEM,) * len(outs),
        scratch_shapes=[lhs_scratch(group)],
        compiler_params=PARAMS,
        name="up_second",
    )(*tables)
    return res[:2], res[2:]


def half_kernel(*refs):
    received, (h_ref, r_ref, p_ref, q_ref) = refs[:ND], refs[ND:]
    me = number()
    for i, offset in enumerate(OFFSETS):
        keep(r_ref, padded(received[i][...]), me ^ offset)
    for j in range(4):
        keep(p_ref, product(load(r_ref, 2 * j + 1), load(r_ref, 2 * j)), j)
    for j in range(2):
        keep(q_ref, product(load(p_ref, 2 * j + 1), load(p_ref, 2 * j)), j)
    h_ref[...] = product(load(q_ref, 1), load(q_ref, 0))[:M]


def half(received):
    return pl.pallas_call(
        half_kernel,
        out_shape=(single(M, 2 * L), halves(ND), halves(4), halves(2)),
        in_specs=[VMEM] * ND,
        out_specs=(VMEM,) * 4,
        compiler_params=PARAMS,
        name="half",
    )(*received)


def pick_kernel(flat_ref, m_ref, rows_ref, buffer_ref, sems):
    unpack_rows(start_rows(flat_ref, buffer_ref, sems), buffer_ref, rows_ref)
    m_ref[...] = unpacked(rows_ref, pl.multiple_of(owned() * L, L))


def pick(flat):
    return pl.pallas_call(
        pick_kernel,
        out_shape=single(L, 2 * L),
        in_specs=[HBM],
        out_specs=VMEM,
        scratch_shapes=[pltpu.VMEM((2, ND * L, L), F32), *ROW_SCRATCH],
        compiler_params=PARAMS,
        name="pick",
    )(in_hbm(flat))


def top_kernel(r_ref, m_ref, p_ref, q_ref, h_ref, other_ref, *refs):
    v_refs, leaf_ref = refs[:ND], refs[ND]
    upper = lax.axis_index("zh") == 1
    own, other = padded(h_ref[...]), padded(other_ref[...])
    h0 = split(jnp.where(upper, other, own))
    h1 = split(jnp.where(upper, own, other))
    misfit = split(adjoint(product(h1, h0) - m_ref[...]))
    left = [jnp.where(upper, a, b) for a, b in zip(h0, misfit)]
    right = [jnp.where(upper, a, b) for a, b in zip(misfit, h1)]
    v = split(product(left, right))
    v0, v1 = split(product(v, load(q_ref, 1))), split(product(load(q_ref, 0), v))
    pairs = (
        product(v0, load(p_ref, 1)),
        product(load(p_ref, 0), v0),
        product(v1, load(p_ref, 3)),
        product(load(p_ref, 2), v1),
    )
    for j in range(4):
        pair = split(pairs[j])
        leaf_ref[2 * j] = product(pair, load(r_ref, 2 * j + 1))[:M]
        leaf_ref[2 * j + 1] = product(load(r_ref, 2 * j), pair)[:M]
    me = number()
    for i, offset in enumerate(OFFSETS):
        v_refs[i][...] = leaf_ref[me ^ offset]


def top(r, m, p, q, h, other):
    return pl.pallas_call(
        top_kernel,
        out_shape=(single(M, 2 * L),) * ND,
        in_specs=[VMEM] * 6,
        out_specs=(VMEM,) * ND,
        scratch_shapes=[pltpu.VMEM((ND, M, 2 * L), F32)],
        compiler_params=PARAMS,
        name="top",
    )(r, m, p, q, h, other)


def quads_down(quads, group, v_refs, ch_ref, tab_ref, tabt_ref, nodes, v_ref, vq_ref, vp_ref):
    columns, rows = scalings(tab_ref, tabt_ref)
    count = len(group)
    place = {f: (n, i) for n, fs in enumerate(UP_GROUPS) for i, f in enumerate(fs)}

    def node(level, j, f):
        n, i = place[f]
        return load(nodes[2 * n + level], j, i)

    for i, f in enumerate(group):
        keep(v_ref, columns(padded(v_refs[i][...]), 7, f), i)
    for quad in quads:
        for i, f in enumerate(group):
            v = load(v_ref, i)
            if quad == 0:
                keep(vq_ref, columns(product(v, node(1, 1, f)), 3, f), 0, i)
            else:
                keep(vq_ref, product(node(1, 0, f), v), 1, i)
    for quad in quads:
        for i, f in enumerate(group):
            v = load(vq_ref, quad, i)
            at = slice(i * L, (i + 1) * L)
            res = columns(product(v, node(0, 2 * quad + 1, f)), 4 * quad + 1, f)
            vp_ref[2 * quad, 0, at], vp_ref[2 * quad, 1, at] = split(res)
            res = product(node(0, 2 * quad, f), v)
            vp_ref[2 * quad + 1, 0, at], vp_ref[2 * quad + 1, 1, at] = split(res)
    out = {}
    for quad in quads:
        for j in (2 * quad, 2 * quad + 1):
            low, up = 2 * j, 2 * j + 1
            res = product(load(vp_ref, j), load(ch_ref, up))
            g_low = g_up = None
            for i, f in enumerate(group):
                at = slice(i * L, (i + 1) * L)
                one = columns(res[at], low, f)
                g_low = one if i == 0 else g_low + one
                one = rows(product(load(ch_ref, low), (vp_ref[j, 0, at], vp_ref[j, 1, at])), low, f)
                g_up = one if i == 0 else g_up + one
            out[low], out[up] = g_low[:M], g_up[:M]
    return out


def down_whole_kernel(group, has_part, *refs):
    count = len(group)
    v_refs, (ch_ref, tab_ref, tabt_ref, *rest) = refs[:count], refs[count:]
    nodes, rest = rest[:NODES], rest[NODES:]
    part_ref = rest.pop(0) if has_part else None
    g_ref, *scratch = rest
    out = quads_down((0, 1), group, v_refs, ch_ref, tab_ref, tabt_ref, nodes, *scratch)
    for k in range(ND):
        g_ref[k] = out[k] + part_ref[k] if has_part else out[k]


def down_last_kernel(mine, group, *refs):
    count = len(group)
    v_refs, (ch_ref, tab_ref, tabt_ref, *rest) = refs[:count], refs[count:]
    nodes, (part_ref, g_ref, *scratch) = rest[:NODES], rest[NODES:]
    core, y = lax.axis_index("c"), lax.axis_index("y")
    for quad in range(2):

        @pl.when(core == (quad if mine else 1 - quad))
        def _():
            out = quads_down((quad,), group, v_refs, ch_ref, tab_ref, tabt_ref, nodes, *scratch)
            for i in range(4):
                g_ref[i ^ y] = out[4 * quad + i] + part_ref[4 * quad + i]


def down(kernel, name, sections, group, v, tables, nodes, *part):
    count = len(group)
    args = (*v, *tables[1:], *nodes, *part)
    return pl.pallas_call(
        kernel,
        out_shape=single(sections, M, 2 * L),
        in_specs=[VMEM] * len(args),
        out_specs=VMEM,
        scratch_shapes=[
            pltpu.VMEM((count, 2, L, 2 * L), BF16),
            pltpu.VMEM((2, count, 2, L, 2 * L), BF16),
            pltpu.VMEM((4, 2, count * L, 2 * L), BF16),
        ],
        compiler_params=PARAMS,
        name=name,
    )(*args)


def sum_kernel(own_ref, a_ref, b_ref, c_ref, out_ref):
    total = (own_ref[...] + a_ref[...]) + (b_ref[...] + c_ref[...])
    out_ref[...] = 2.0 * adjoint(padded(total))[:M]


def sum_up(own, a, b, c):
    return pl.pallas_call(
        sum_kernel,
        out_shape=single(M, 2 * L),
        in_specs=[VMEM] * 4,
        out_specs=VMEM,
        compiler_params=PARAMS,
        name="sum_up",
    )(own, a, b, c)


def store_kernel(*refs):
    parts, (out_ref, rows_ref, buffer_ref, sems) = refs[:ND], refs[ND:]
    core, y = lax.axis_index("c"), lax.axis_index("y")
    for i in range(ND):
        place = (4 * core if i < 4 else 4 * (1 - core)) + (y ^ (i % 4))
        at = pl.ds(pl.multiple_of(place * L, L), M)
        rows_ref[0, at, :] = parts[i][:, :L]
        rows_ref[1, at, :] = parts[i][:, L:]
    copies = []
    for i, (a, b) in enumerate(ROWS):
        for m in range(a, b):
            rows = pl.ds(m, ND, stride=L)
            buffer_ref[:, m * W : m * W + M] = rows_ref[0, rows, :][:, :M]
            buffer_ref[:, m * W + M : (m + 1) * W] = rows_ref[1, rows, :][:, :M]
        at = (slice(None), pl.ds(a * W, (b - a) * W))
        copies.append(pltpu.make_async_copy(buffer_ref.at[at], out_ref.at[at], sems.at[i]))
        copies[-1].start()
    for copy in copies:
        copy.wait()


def store(parts):
    return pl.pallas_call(
        store_kernel,
        out_shape=single(ND, M * W),
        in_specs=[VMEM] * ND,
        out_specs=HBM,
        scratch_shapes=[pltpu.VMEM((2, ND * L, L), F32), *ROW_SCRATCH],
        compiler_params=PARAMS,
        name="store",
    )(*parts)


def shards(coupling, propagation, frequency_offset, measured):
    swap = [(0, 1), (1, 0)]

    def exchange(i, x):
        return lax.ppermute(x, ("zl", "x"), [(s, s ^ OFFSETS[i]) for s in range(ND)]) if OFFSETS[i] else x

    def turned(i, x):
        return lax.ppermute(x, "y", [(s, s ^ i) for s in range(4)])

    tables, nodes_first, a_first = up(UP_GROUPS[0], frequency_offset, propagation, coupling)
    nodes_second, a_second = up_second(UP_GROUPS[1], tables)
    nodes, a = (*nodes_first, *nodes_second), (*a_first, *a_second)
    h, r, p, q = half([exchange(i, x) for i, x in enumerate(a)])
    other = lax.ppermute(h, ("zh", "zl"), [(0, 3), (1, 2), (2, 1), (3, 0)])
    v = top(r, pick(measured), p, q, h, other)
    v = [exchange(i, x) for i, x in enumerate(v)]

    one, two = DOWN_GROUPS
    part = down(functools.partial(down_whole_kernel, one, False), "down_1", ND, one, [v[i] for i in one], tables, nodes)
    last = [v[i] for i in two]
    theirs = down(functools.partial(down_last_kernel, False, two), "down_theirs", 4, two, last, tables, nodes, part)
    received = lax.ppermute(theirs, "c", swap)
    mine = down(functools.partial(down_last_kernel, True, two), "down_mine", 4, two, last, tables, nodes, part)

    g = mine + received
    total = sum_up(g[0], *[turned(i, g[i]) for i in range(1, 4)])
    parts = [total] + [turned(i, total) for i in range(1, 4)]
    parts += [lax.ppermute(x, "c", swap) for x in parts]
    return store(parts)


def solution(mesh):
    fine = Mesh(mesh.devices.reshape(2, 2, 4, 4, 2), ("zh", "zl", "x", "y", "c"))
    sec, freq = ("zh", "zl", "x"), ("y", "c")
    return jax.shard_map(
        shards,
        mesh=fine,
        in_specs=(P(sec, None), P(sec, None), P(freq), P(freq, None)),
        out_specs=P(sec, None),
        check_vma=False,
    )
```

```python
import functools

import jax
import jax.numpy as jnp
from jax import lax
from jax.experimental import pallas as pl
from jax.experimental.pallas import tpu as pltpu
from jax.sharding import Mesh, PartitionSpec as P

M = 120
W = 2 * M
L = 128
ND = 8
F32, BF16 = jnp.float32, jnp.bfloat16
PARAMS = pltpu.CompilerParams(vmem_limit_bytes=20 * 1024 * 1024)
VMEM = pl.BlockSpec(memory_space=pltpu.VMEM)
SMEM = pl.BlockSpec(memory_space=pltpu.SMEM)
HBM = pl.BlockSpec(memory_space=pltpu.HBM)

OFFSETS = (2, 6, 4, 7, 3, 5, 1, 0)
UP_GROUPS = ((0, 1, 2), (3, 4, 5, 6, 7))
DOWN_GROUPS = ((7, 0, 1), (2, 3, 4, 5, 6))
NODES = 2 * len(UP_GROUPS)
ROWS = ((0, 32), (32, 64), (64, 96), (96, 120))


def single(*dims):
    return jax.ShapeDtypeStruct(dims, F32)


def halves(*dims):
    return jax.ShapeDtypeStruct((*dims, 2, L, 2 * L), BF16)


def split(x):
    high = x.astype(BF16)
    return high, (x - high.astype(F32)).astype(BF16)


def right_form(x):
    real, imag = x[:, :L], x[:, L:]
    return jnp.concatenate([x, jnp.concatenate([-imag, real], axis=1)], axis=0)


def product(left, right):
    (left_high, left_low), (right_high, right_low) = left, right
    right_high, right_low = right_form(right_high), right_form(right_low)
    return jnp.dot(
        jnp.concatenate([left_high, left_low, left_high], axis=1),
        jnp.concatenate([right_high, right_high, right_low], axis=0),
        preferred_element_type=F32,
    )


def load(ref, *at):
    return ref[(*at, 0)], ref[(*at, 1)]


def keep(ref, x, *at):
    ref[(*at, 0)], ref[(*at, 1)] = split(x)


def scaled(x, cosine, sine):
    real, imag = x[:, :L], x[:, L:]
    return jnp.concatenate([cosine * real - sine * imag, cosine * imag + sine * real], axis=1)


def adjoint(x):
    return jnp.concatenate([x[:, :L].T, -x[:, L:].T], axis=1)


def padded(x):
    return jnp.concatenate([x, jnp.zeros((L - M, 2 * L), F32)], axis=0)


def start_rows(flat_ref, buffer_ref, sems):
    copies = []
    for i, (a, b) in enumerate(ROWS):
        at = (slice(None), pl.ds(a * W, (b - a) * W))
        copies.append(pltpu.make_async_copy(flat_ref.at[at], buffer_ref.at[at], sems.at[i]))
        copies[-1].start()
    return copies


def unpack_rows(copies, buffer_ref, out_ref):
    zeros = jnp.zeros((ND, L - M), F32)
    for (a, b), copy in zip(ROWS, copies):
        copy.wait()
        for part in range(2):
            for start in range(a, b, ND):
                firsts = [m * W + part * M for m in range(start, start + ND)]
                rows = [jnp.concatenate([buffer_ref[:, i : i + M], zeros], axis=1) for i in firsts]
                block = jnp.swapaxes(jnp.stack(rows), 0, 1)
                for k in range(ND):
                    out_ref[part, k * L + start : k * L + start + ND, :] = block[k]
    for k in range(ND):
        out_ref[:, k * L + M : (k + 1) * L, :] = jnp.zeros((2, L - M, L), F32)


def unpacked(rows_ref, start):
    return jnp.concatenate([rows_ref[0, pl.ds(start, L), :], rows_ref[1, pl.ds(start, L), :]], axis=1)


ROW_SCRATCH = [pltpu.VMEM((ND, M * W), F32), pltpu.SemaphoreType.DMA((len(ROWS),))]


def number():
    return lax.axis_index("zl") * 4 + lax.axis_index("x")


def owned():
    return number() ^ (lax.axis_index("zh") * 4)


def scalings(tab_ref, tabt_ref):
    def columns(x, k, f):
        i = f * ND + k
        return scaled(x, tab_ref[0, i : i + 1, :], tab_ref[1, i : i + 1, :])

    def rows(x, k, f):
        i = f * ND + k
        return scaled(x, tabt_ref[0, :, i : i + 1], tabt_ref[1, :, i : i + 1])

    return columns, rows


def up_group(group, a_refs, c_ref, ch_ref, tab_ref, tabt_ref, p_ref, q_ref, lhs_ref):
    columns, rows = scalings(tab_ref, tabt_ref)
    count = len(group)
    for j in range(4):
        low, up = 2 * j, 2 * j + 1
        c_up = unpacked(c_ref, up * L)
        for i, f in enumerate(group):
            at = slice(i * L, (i + 1) * L)
            lhs_ref[j, 0, at], lhs_ref[j, 1, at] = split(columns(c_up, low, f))
        res = product(load(lhs_ref, j), load(ch_ref, low))
        for i, f in enumerate(group):
            one = res[i * L : (i + 1) * L]
            keep(p_ref, rows(one, up, f) if j % 2 == 0 else one, j, i)
    for i, f in enumerate(group):
        keep(q_ref, rows(product(load(p_ref, 1, i), load(p_ref, 0, i)), 3, f), 0, i)
    for i, f in enumerate(group):
        keep(q_ref, product(load(p_ref, 3, i), load(p_ref, 2, i)), 1, i)
    for i, f in enumerate(group):
        a_refs[i][...] = rows(product(load(q_ref, 1, i), load(q_ref, 0, i)), 7, f)[:M]


def up_kernel(group, freq_hbm, prop_hbm, flat_hbm, c_ref, ch_ref, tab_ref, tabt_ref, p_ref, q_ref, *refs):
    count = len(group)
    a_refs, (lhs_ref, freq_ref, prop_ref, small, buffer_ref, sems) = refs[:count], refs[count:]
    first = pltpu.make_async_copy(freq_hbm, freq_ref, small.at[0])
    second = pltpu.make_async_copy(prop_hbm, prop_ref, small.at[1])
    first.start()
    second.start()
    copies = start_rows(flat_hbm, buffer_ref, sems)
    tab_ref[...] = jnp.zeros(tab_ref.shape, F32)
    first.wait()
    second.wait()
    for f in range(ND):
        phase = prop_ref[...] * freq_ref[owned() ^ OFFSETS[f]]
        tab_ref[0, f * ND : (f + 1) * ND, 0:M] = jnp.cos(phase)
        tab_ref[1, f * ND : (f + 1) * ND, 0:M] = jnp.sin(phase)
    tabt_ref[0] = tab_ref[0].T
    tabt_ref[1] = tab_ref[1].T
    unpack_rows(copies, buffer_ref, c_ref)
    for k in range(ND):
        keep(ch_ref, unpacked(c_ref, k * L), k)
    up_group(group, a_refs, c_ref, ch_ref, tab_ref, tabt_ref, p_ref, q_ref, lhs_ref)


def up_second_kernel(group, c_ref, ch_ref, tab_ref, tabt_ref, p_ref, q_ref, *refs):
    a_refs, (lhs_ref,) = refs[: len(group)], refs[len(group) :]
    up_group(group, a_refs, c_ref, ch_ref, tab_ref, tabt_ref, p_ref, q_ref, lhs_ref)


def up_outs(group):
    count = len(group)
    return (halves(4, count), halves(2, count)) + (single(M, 2 * L),) * count


def lhs_scratch(group):
    return pltpu.VMEM((4, 2, len(group) * L, 2 * L), BF16)


def in_hbm(x):
    return pltpu.with_memory_space_constraint(x, pltpu.HBM)


def up(group, freq, prop, flat):
    tables = (single(2, ND * L, L), halves(ND), single(2, ND * ND, L), single(2, L, ND * ND))
    outs = tables + up_outs(group)
    res = pl.pallas_call(
        functools.partial(up_kernel, group),
        out_shape=outs,
        in_specs=[HBM, HBM, HBM],
        out_specs=(VMEM,) * len(outs),
        scratch_shapes=[
            lhs_scratch(group),
            pltpu.SMEM((ND,), F32),
            pltpu.VMEM((ND, M), F32),
            pltpu.SemaphoreType.DMA((2,)),
            *ROW_SCRATCH,
        ],
        compiler_params=PARAMS,
        name="up",
    )(in_hbm(freq), in_hbm(prop), in_hbm(flat))
    return res[:4], res[4:6], res[6:]


def up_second(group, tables):
    outs = up_outs(group)
    res = pl.pallas_call(
        functools.partial(up_second_kernel, group),
        out_shape=outs,
        in_specs=[VMEM] * 4,
        out_specs=(VMEM,) * len(outs),
        scratch_shapes=[lhs_scratch(group)],
        compiler_params=PARAMS,
        name="up_second",
    )(*tables)
    return res[:2], res[2:]


def half_kernel(*refs):
    received, (h_ref, r_ref, p_ref, q_ref) = refs[:ND], refs[ND:]
    me = number()
    for i, offset in enumerate(OFFSETS):
        keep(r_ref, padded(received[i][...]), me ^ offset)
    for j in range(4):
        keep(p_ref, product(load(r_ref, 2 * j + 1), load(r_ref, 2 * j)), j)
    for j in range(2):
        keep(q_ref, product(load(p_ref, 2 * j + 1), load(p_ref, 2 * j)), j)
    h_ref[...] = product(load(q_ref, 1), load(q_ref, 0))[:M]


def half(received):
    return pl.pallas_call(
        half_kernel,
        out_shape=(single(M, 2 * L), halves(ND), halves(4), halves(2)),
        in_specs=[VMEM] * ND,
        out_specs=(VMEM,) * 4,
        compiler_params=PARAMS,
        name="half",
    )(*received)


def pick_kernel(flat_ref, m_ref, rows_ref, buffer_ref, sems):
    unpack_rows(start_rows(flat_ref, buffer_ref, sems), buffer_ref, rows_ref)
    m_ref[...] = unpacked(rows_ref, pl.multiple_of(owned() * L, L))


def pick(flat):
    return pl.pallas_call(
        pick_kernel,
        out_shape=single(L, 2 * L),
        in_specs=[HBM],
        out_specs=VMEM,
        scratch_shapes=[pltpu.VMEM((2, ND * L, L), F32), *ROW_SCRATCH],
        compiler_params=PARAMS,
        name="pick",
    )(in_hbm(flat))


def top_kernel(r_ref, m_ref, p_ref, q_ref, h_ref, other_ref, *refs):
    v_refs, leaf_ref = refs[:ND], refs[ND]
    upper = lax.axis_index("zh") == 1
    own, other = padded(h_ref[...]), padded(other_ref[...])
    h0 = split(jnp.where(upper, other, own))
    h1 = split(jnp.where(upper, own, other))
    misfit = split(adjoint(product(h1, h0) - m_ref[...]))
    left = [jnp.where(upper, a, b) for a, b in zip(h0, misfit)]
    right = [jnp.where(upper, a, b) for a, b in zip(misfit, h1)]
    v = split(product(left, right))
    v0, v1 = split(product(v, load(q_ref, 1))), split(product(load(q_ref, 0), v))
    pairs = (
        product(v0, load(p_ref, 1)),
        product(load(p_ref, 0), v0),
        product(v1, load(p_ref, 3)),
        product(load(p_ref, 2), v1),
    )
    for j in range(4):
        pair = split(pairs[j])
        leaf_ref[2 * j] = product(pair, load(r_ref, 2 * j + 1))[:M]
        leaf_ref[2 * j + 1] = product(load(r_ref, 2 * j), pair)[:M]
    me = number()
    for i, offset in enumerate(OFFSETS):
        v_refs[i][...] = leaf_ref[me ^ offset]


def top(r, m, p, q, h, other):
    return pl.pallas_call(
        top_kernel,
        out_shape=(single(M, 2 * L),) * ND,
        in_specs=[VMEM] * 6,
        out_specs=(VMEM,) * ND,
        scratch_shapes=[pltpu.VMEM((ND, M, 2 * L), F32)],
        compiler_params=PARAMS,
        name="top",
    )(r, m, p, q, h, other)


def quads_down(quads, group, v_refs, ch_ref, tab_ref, tabt_ref, nodes, v_ref, vq_ref, vp_ref):
    columns, rows = scalings(tab_ref, tabt_ref)
    count = len(group)
    place = {f: (n, i) for n, fs in enumerate(UP_GROUPS) for i, f in enumerate(fs)}

    def node(level, j, f):
        n, i = place[f]
        return load(nodes[2 * n + level], j, i)

    for i, f in enumerate(group):
        keep(v_ref, columns(padded(v_refs[i][...]), 7, f), i)
    for quad in quads:
        for i, f in enumerate(group):
            v = load(v_ref, i)
            if quad == 0:
                keep(vq_ref, columns(product(v, node(1, 1, f)), 3, f), 0, i)
            else:
                keep(vq_ref, product(node(1, 0, f), v), 1, i)
    for quad in quads:
        for i, f in enumerate(group):
            v = load(vq_ref, quad, i)
            at = slice(i * L, (i + 1) * L)
            res = columns(product(v, node(0, 2 * quad + 1, f)), 4 * quad + 1, f)
            vp_ref[2 * quad, 0, at], vp_ref[2 * quad, 1, at] = split(res)
            res = product(node(0, 2 * quad, f), v)
            vp_ref[2 * quad + 1, 0, at], vp_ref[2 * quad + 1, 1, at] = split(res)
    out = {}
    for quad in quads:
        for j in (2 * quad, 2 * quad + 1):
            low, up = 2 * j, 2 * j + 1
            res = product(load(vp_ref, j), load(ch_ref, up))
            g_low = g_up = None
            for i, f in enumerate(group):
                at = slice(i * L, (i + 1) * L)
                one = columns(res[at], low, f)
                g_low = one if i == 0 else g_low + one
                one = rows(product(load(ch_ref, low), (vp_ref[j, 0, at], vp_ref[j, 1, at])), low, f)
                g_up = one if i == 0 else g_up + one
            out[low], out[up] = g_low[:M], g_up[:M]
    return out


def down_whole_kernel(group, has_part, *refs):
    count = len(group)
    v_refs, (ch_ref, tab_ref, tabt_ref, *rest) = refs[:count], refs[count:]
    nodes, rest = rest[:NODES], rest[NODES:]
    part_ref = rest.pop(0) if has_part else None
    g_ref, *scratch = rest
    out = quads_down((0, 1), group, v_refs, ch_ref, tab_ref, tabt_ref, nodes, *scratch)
    for k in range(ND):
        g_ref[k] = out[k] + part_ref[k] if has_part else out[k]


def down_last_kernel(mine, group, *refs):
    count = len(group)
    v_refs, (ch_ref, tab_ref, tabt_ref, *rest) = refs[:count], refs[count:]
    nodes, (part_ref, g_ref, *scratch) = rest[:NODES], rest[NODES:]
    core, y = lax.axis_index("c"), lax.axis_index("y")
    for quad in range(2):

        @pl.when(core == (quad if mine else 1 - quad))
        def _():
            out = quads_down((quad,), group, v_refs, ch_ref, tab_ref, tabt_ref, nodes, *scratch)
            for i in range(4):
                g_ref[i ^ y] = out[4 * quad + i] + part_ref[4 * quad + i]


def down(kernel, name, sections, group, v, tables, nodes, *part):
    count = len(group)
    args = (*v, *tables[1:], *nodes, *part)
    return pl.pallas_call(
        kernel,
        out_shape=single(sections, M, 2 * L),
        in_specs=[VMEM] * len(args),
        out_specs=VMEM,
        scratch_shapes=[
            pltpu.VMEM((count, 2, L, 2 * L), BF16),
            pltpu.VMEM((2, count, 2, L, 2 * L), BF16),
            pltpu.VMEM((4, 2, count * L, 2 * L), BF16),
        ],
        compiler_params=PARAMS,
        name=name,
    )(*args)


def sum_kernel(own_ref, a_ref, b_ref, c_ref, out_ref):
    total = (own_ref[...] + a_ref[...]) + (b_ref[...] + c_ref[...])
    out_ref[...] = 2.0 * adjoint(padded(total))[:M]


def sum_up(own, a, b, c):
    return pl.pallas_call(
        sum_kernel,
        out_shape=single(M, 2 * L),
        in_specs=[VMEM] * 4,
        out_specs=VMEM,
        compiler_params=PARAMS,
        name="sum_up",
    )(own, a, b, c)


def store_kernel(*refs):
    parts, (out_ref, rows_ref, buffer_ref, sems) = refs[:ND], refs[ND:]
    core, y = lax.axis_index("c"), lax.axis_index("y")
    for i in range(ND):
        place = (4 * core if i < 4 else 4 * (1 - core)) + (y ^ (i % 4))
        at = pl.ds(pl.multiple_of(place * L, L), M)
        rows_ref[0, at, :] = parts[i][:, :L]
        rows_ref[1, at, :] = parts[i][:, L:]
    copies = []
    for i, (a, b) in enumerate(ROWS):
        for m in range(a, b):
            rows = pl.ds(m, ND, stride=L)
            buffer_ref[:, m * W : m * W + M] = rows_ref[0, rows, :][:, :M]
            buffer_ref[:, m * W + M : (m + 1) * W] = rows_ref[1, rows, :][:, :M]
        at = (slice(None), pl.ds(a * W, (b - a) * W))
        copies.append(pltpu.make_async_copy(buffer_ref.at[at], out_ref.at[at], sems.at[i]))
        copies[-1].start()
    for copy in copies:
        copy.wait()


def store(parts):
    return pl.pallas_call(
        store_kernel,
        out_shape=single(ND, M * W),
        in_specs=[VMEM] * ND,
        out_specs=HBM,
        scratch_shapes=[pltpu.VMEM((2, ND * L, L), F32), *ROW_SCRATCH],
        compiler_params=PARAMS,
        name="store",
    )(*parts)


def shards(coupling, propagation, frequency_offset, measured):
    swap = [(0, 1), (1, 0)]

    def exchange(i, x):
        return lax.ppermute(x, ("zl", "x"), [(s, s ^ OFFSETS[i]) for s in range(ND)]) if OFFSETS[i] else x

    def turned(i, x):
        return lax.ppermute(x, "y", [(s, s ^ i) for s in range(4)])

    tables, nodes_first, a_first = up(UP_GROUPS[0], frequency_offset, propagation, coupling)
    nodes_second, a_second = up_second(UP_GROUPS[1], tables)
    nodes, a = (*nodes_first, *nodes_second), (*a_first, *a_second)
    h, r, p, q = half([exchange(i, x) for i, x in enumerate(a)])
    other = lax.ppermute(h, ("zh", "zl"), [(0, 3), (1, 2), (2, 1), (3, 0)])
    v = top(r, pick(measured), p, q, h, other)
    v = [exchange(i, x) for i, x in enumerate(v)]

    one, two = DOWN_GROUPS
    part = down(functools.partial(down_whole_kernel, one, False), "down_1", ND, one, [v[i] for i in one], tables, nodes)
    last = [v[i] for i in two]
    theirs = down(functools.partial(down_last_kernel, False, two), "down_theirs", 4, two, last, tables, nodes, part)
    received = lax.ppermute(theirs, "c", swap)
    mine = down(functools.partial(down_last_kernel, True, two), "down_mine", 4, two, last, tables, nodes, part)

    g = mine + received
    order = (3, 1, 2)
    total = sum_up(g[0], *[turned(i, g[i]) for i in order])
    turns = {i: turned(i, total) for i in order}
    parts = [total] + [turns[i] for i in (1, 2, 3)]
    parts += [lax.ppermute(x, "c", swap) for x in parts]
    return store(parts)


def solution(mesh):
    fine = Mesh(mesh.devices.reshape(2, 2, 4, 4, 2), ("zh", "zl", "x", "y", "c"))
    sec, freq = ("zh", "zl", "x"), ("y", "c")
    return jax.shard_map(
        shards,
        mesh=fine,
        in_specs=(P(sec, None), P(sec, None), P(freq), P(freq, None)),
        out_specs=P(sec, None),
        check_vma=False,
    )
```

```python
import functools

import jax
import jax.numpy as jnp
from jax import lax
from jax.experimental import pallas as pl
from jax.experimental.pallas import tpu as pltpu
from jax.sharding import Mesh, PartitionSpec as P

M = 120
W = 2 * M
L = 128
ND = 8
F32, BF16 = jnp.float32, jnp.bfloat16
PARAMS = pltpu.CompilerParams(vmem_limit_bytes=20 * 1024 * 1024)
VMEM = pl.BlockSpec(memory_space=pltpu.VMEM)
SMEM = pl.BlockSpec(memory_space=pltpu.SMEM)
HBM = pl.BlockSpec(memory_space=pltpu.HBM)

OFFSETS = (2, 6, 4, 7, 3, 5, 1, 0)
UP_GROUPS = ((0, 1, 2), (3, 4, 5, 6, 7))
DOWN_GROUPS = ((7, 0), (1, 2, 3, 4, 5, 6))
NODES = 2 * len(UP_GROUPS)
ROWS = ((0, 32), (32, 64), (64, 96), (96, 120))


def single(*dims):
    return jax.ShapeDtypeStruct(dims, F32)


def halves(*dims):
    return jax.ShapeDtypeStruct((*dims, 2, L, 2 * L), BF16)


def split(x):
    high = x.astype(BF16)
    return high, (x - high.astype(F32)).astype(BF16)


def right_form(x):
    real, imag = x[:, :L], x[:, L:]
    return jnp.concatenate([x, jnp.concatenate([-imag, real], axis=1)], axis=0)


def product(left, right):
    (left_high, left_low), (right_high, right_low) = left, right
    right_high, right_low = right_form(right_high), right_form(right_low)
    return jnp.dot(
        jnp.concatenate([left_high, left_low, left_high], axis=1),
        jnp.concatenate([right_high, right_high, right_low], axis=0),
        preferred_element_type=F32,
    )


def load(ref, *at):
    return ref[(*at, 0)], ref[(*at, 1)]


def keep(ref, x, *at):
    ref[(*at, 0)], ref[(*at, 1)] = split(x)


def scaled(x, cosine, sine):
    real, imag = x[:, :L], x[:, L:]
    return jnp.concatenate([cosine * real - sine * imag, cosine * imag + sine * real], axis=1)


def adjoint(x):
    return jnp.concatenate([x[:, :L].T, -x[:, L:].T], axis=1)


def padded(x):
    return jnp.concatenate([x, jnp.zeros((L - M, 2 * L), F32)], axis=0)


def start_rows(flat_ref, buffer_ref, sems):
    copies = []
    for i, (a, b) in enumerate(ROWS):
        at = (slice(None), pl.ds(a * W, (b - a) * W))
        copies.append(pltpu.make_async_copy(flat_ref.at[at], buffer_ref.at[at], sems.at[i]))
        copies[-1].start()
    return copies


def unpack_rows(copies, buffer_ref, out_ref):
    zeros = jnp.zeros((ND, L - M), F32)
    for (a, b), copy in zip(ROWS, copies):
        copy.wait()
        for part in range(2):
            for start in range(a, b, ND):
                firsts = [m * W + part * M for m in range(start, start + ND)]
                rows = [jnp.concatenate([buffer_ref[:, i : i + M], zeros], axis=1) for i in firsts]
                block = jnp.swapaxes(jnp.stack(rows), 0, 1)
                for k in range(ND):
                    out_ref[part, k * L + start : k * L + start + ND, :] = block[k]
    for k in range(ND):
        out_ref[:, k * L + M : (k + 1) * L, :] = jnp.zeros((2, L - M, L), F32)


def unpacked(rows_ref, start):
    return jnp.concatenate([rows_ref[0, pl.ds(start, L), :], rows_ref[1, pl.ds(start, L), :]], axis=1)


ROW_SCRATCH = [pltpu.VMEM((ND, M * W), F32), pltpu.SemaphoreType.DMA((len(ROWS),))]


def number():
    return lax.axis_index("zl") * 4 + lax.axis_index("x")


def owned():
    return number() ^ (lax.axis_index("zh") * 4)


def scalings(tab_ref, tabt_ref):
    def columns(x, k, f):
        i = f * ND + k
        return scaled(x, tab_ref[0, i : i + 1, :], tab_ref[1, i : i + 1, :])

    def rows(x, k, f):
        i = f * ND + k
        return scaled(x, tabt_ref[0, :, i : i + 1], tabt_ref[1, :, i : i + 1])

    return columns, rows


def up_group(group, a_refs, c_ref, ch_ref, tab_ref, tabt_ref, p_ref, q_ref, lhs_ref):
    columns, rows = scalings(tab_ref, tabt_ref)
    count = len(group)
    for j in range(4):
        low, up = 2 * j, 2 * j + 1
        c_up = unpacked(c_ref, up * L)
        for i, f in enumerate(group):
            at = slice(i * L, (i + 1) * L)
            lhs_ref[j, 0, at], lhs_ref[j, 1, at] = split(columns(c_up, low, f))
        res = product(load(lhs_ref, j), load(ch_ref, low))
        for i, f in enumerate(group):
            one = res[i * L : (i + 1) * L]
            keep(p_ref, rows(one, up, f) if j % 2 == 0 else one, j, i)
    for i, f in enumerate(group):
        keep(q_ref, rows(product(load(p_ref, 1, i), load(p_ref, 0, i)), 3, f), 0, i)
    for i, f in enumerate(group):
        keep(q_ref, product(load(p_ref, 3, i), load(p_ref, 2, i)), 1, i)
    for i, f in enumerate(group):
        a_refs[i][...] = rows(product(load(q_ref, 1, i), load(q_ref, 0, i)), 7, f)[:M]


def up_kernel(group, freq_hbm, prop_hbm, flat_hbm, c_ref, ch_ref, tab_ref, tabt_ref, p_ref, q_ref, *refs):
    count = len(group)
    a_refs, (lhs_ref, freq_ref, prop_ref, small, buffer_ref, sems) = refs[:count], refs[count:]
    first = pltpu.make_async_copy(freq_hbm, freq_ref, small.at[0])
    second = pltpu.make_async_copy(prop_hbm, prop_ref, small.at[1])
    first.start()
    second.start()
    copies = start_rows(flat_hbm, buffer_ref, sems)
    tab_ref[...] = jnp.zeros(tab_ref.shape, F32)
    first.wait()
    second.wait()
    for f in range(ND):
        phase = prop_ref[...] * freq_ref[owned() ^ OFFSETS[f]]
        tab_ref[0, f * ND : (f + 1) * ND, 0:M] = jnp.cos(phase)
        tab_ref[1, f * ND : (f + 1) * ND, 0:M] = jnp.sin(phase)
    tabt_ref[0] = tab_ref[0].T
    tabt_ref[1] = tab_ref[1].T
    unpack_rows(copies, buffer_ref, c_ref)
    for k in range(ND):
        keep(ch_ref, unpacked(c_ref, k * L), k)
    up_group(group, a_refs, c_ref, ch_ref, tab_ref, tabt_ref, p_ref, q_ref, lhs_ref)


def up_second_kernel(group, c_ref, ch_ref, tab_ref, tabt_ref, p_ref, q_ref, *refs):
    a_refs, (lhs_ref,) = refs[: len(group)], refs[len(group) :]
    up_group(group, a_refs, c_ref, ch_ref, tab_ref, tabt_ref, p_ref, q_ref, lhs_ref)


def up_outs(group):
    count = len(group)
    return (halves(4, count), halves(2, count)) + (single(M, 2 * L),) * count


def lhs_scratch(group):
    return pltpu.VMEM((4, 2, len(group) * L, 2 * L), BF16)


def in_hbm(x):
    return pltpu.with_memory_space_constraint(x, pltpu.HBM)


def up(group, freq, prop, flat):
    tables = (single(2, ND * L, L), halves(ND), single(2, ND * ND, L), single(2, L, ND * ND))
    outs = tables + up_outs(group)
    res = pl.pallas_call(
        functools.partial(up_kernel, group),
        out_shape=outs,
        in_specs=[HBM, HBM, HBM],
        out_specs=(VMEM,) * len(outs),
        scratch_shapes=[
            lhs_scratch(group),
            pltpu.SMEM((ND,), F32),
            pltpu.VMEM((ND, M), F32),
            pltpu.SemaphoreType.DMA((2,)),
            *ROW_SCRATCH,
        ],
        compiler_params=PARAMS,
        name="up",
    )(in_hbm(freq), in_hbm(prop), in_hbm(flat))
    return res[:4], res[4:6], res[6:]


def up_second(group, tables):
    outs = up_outs(group)
    res = pl.pallas_call(
        functools.partial(up_second_kernel, group),
        out_shape=outs,
        in_specs=[VMEM] * 4,
        out_specs=(VMEM,) * len(outs),
        scratch_shapes=[lhs_scratch(group)],
        compiler_params=PARAMS,
        name="up_second",
    )(*tables)
    return res[:2], res[2:]


def half_kernel(*refs):
    received, (h_ref, r_ref, p_ref, q_ref) = refs[:ND], refs[ND:]
    me = number()
    for i, offset in enumerate(OFFSETS):
        keep(r_ref, padded(received[i][...]), me ^ offset)
    for j in range(4):
        keep(p_ref, product(load(r_ref, 2 * j + 1), load(r_ref, 2 * j)), j)
    for j in range(2):
        keep(q_ref, product(load(p_ref, 2 * j + 1), load(p_ref, 2 * j)), j)
    h_ref[...] = product(load(q_ref, 1), load(q_ref, 0))[:M]


def half(received):
    return pl.pallas_call(
        half_kernel,
        out_shape=(single(M, 2 * L), halves(ND), halves(4), halves(2)),
        in_specs=[VMEM] * ND,
        out_specs=(VMEM,) * 4,
        compiler_params=PARAMS,
        name="half",
    )(*received)


def pick_kernel(flat_ref, m_ref, rows_ref, buffer_ref, sems):
    unpack_rows(start_rows(flat_ref, buffer_ref, sems), buffer_ref, rows_ref)
    m_ref[...] = unpacked(rows_ref, pl.multiple_of(owned() * L, L))


def pick(flat):
    return pl.pallas_call(
        pick_kernel,
        out_shape=single(L, 2 * L),
        in_specs=[HBM],
        out_specs=VMEM,
        scratch_shapes=[pltpu.VMEM((2, ND * L, L), F32), *ROW_SCRATCH],
        compiler_params=PARAMS,
        name="pick",
    )(in_hbm(flat))


def top_kernel(r_ref, m_ref, p_ref, q_ref, h_ref, other_ref, *refs):
    v_refs, leaf_ref = refs[:ND], refs[ND]
    upper = lax.axis_index("zh") == 1
    own, other = padded(h_ref[...]), padded(other_ref[...])
    h0 = split(jnp.where(upper, other, own))
    h1 = split(jnp.where(upper, own, other))
    misfit = split(adjoint(product(h1, h0) - m_ref[...]))
    left = [jnp.where(upper, a, b) for a, b in zip(h0, misfit)]
    right = [jnp.where(upper, a, b) for a, b in zip(misfit, h1)]
    v = split(product(left, right))
    v0, v1 = split(product(v, load(q_ref, 1))), split(product(load(q_ref, 0), v))
    pairs = (
        product(v0, load(p_ref, 1)),
        product(load(p_ref, 0), v0),
        product(v1, load(p_ref, 3)),
        product(load(p_ref, 2), v1),
    )
    for j in range(4):
        pair = split(pairs[j])
        leaf_ref[2 * j] = product(pair, load(r_ref, 2 * j + 1))[:M]
        leaf_ref[2 * j + 1] = product(load(r_ref, 2 * j), pair)[:M]
    me = number()
    for i, offset in enumerate(OFFSETS):
        v_refs[i][...] = leaf_ref[me ^ offset]


def top(r, m, p, q, h, other):
    return pl.pallas_call(
        top_kernel,
        out_shape=(single(M, 2 * L),) * ND,
        in_specs=[VMEM] * 6,
        out_specs=(VMEM,) * ND,
        scratch_shapes=[pltpu.VMEM((ND, M, 2 * L), F32)],
        compiler_params=PARAMS,
        name="top",
    )(r, m, p, q, h, other)


def quads_down(quads, group, v_refs, ch_ref, tab_ref, tabt_ref, nodes, v_ref, vq_ref, vp_ref):
    columns, rows = scalings(tab_ref, tabt_ref)
    count = len(group)
    place = {f: (n, i) for n, fs in enumerate(UP_GROUPS) for i, f in enumerate(fs)}

    def node(level, j, f):
        n, i = place[f]
        return load(nodes[2 * n + level], j, i)

    for i, f in enumerate(group):
        keep(v_ref, columns(padded(v_refs[i][...]), 7, f), i)
    for quad in quads:
        for i, f in enumerate(group):
            v = load(v_ref, i)
            if quad == 0:
                keep(vq_ref, columns(product(v, node(1, 1, f)), 3, f), 0, i)
            else:
                keep(vq_ref, product(node(1, 0, f), v), 1, i)
    for quad in quads:
        for i, f in enumerate(group):
            v = load(vq_ref, quad, i)
            at = slice(i * L, (i + 1) * L)
            res = columns(product(v, node(0, 2 * quad + 1, f)), 4 * quad + 1, f)
            vp_ref[2 * quad, 0, at], vp_ref[2 * quad, 1, at] = split(res)
            res = product(node(0, 2 * quad, f), v)
            vp_ref[2 * quad + 1, 0, at], vp_ref[2 * quad + 1, 1, at] = split(res)
    out = {}
    for quad in quads:
        for j in (2 * quad, 2 * quad + 1):
            low, up = 2 * j, 2 * j + 1
            res = product(load(vp_ref, j), load(ch_ref, up))
            g_low = g_up = None
            for i, f in enumerate(group):
                at = slice(i * L, (i + 1) * L)
                one = columns(res[at], low, f)
                g_low = one if i == 0 else g_low + one
                one = rows(product(load(ch_ref, low), (vp_ref[j, 0, at], vp_ref[j, 1, at])), low, f)
                g_up = one if i == 0 else g_up + one
            out[low], out[up] = g_low[:M], g_up[:M]
    return out


def down_whole_kernel(group, has_part, *refs):
    count = len(group)
    v_refs, (ch_ref, tab_ref, tabt_ref, *rest) = refs[:count], refs[count:]
    nodes, rest = rest[:NODES], rest[NODES:]
    part_ref = rest.pop(0) if has_part else None
    g_ref, *scratch = rest
    out = quads_down((0, 1), group, v_refs, ch_ref, tab_ref, tabt_ref, nodes, *scratch)
    for k in range(ND):
        g_ref[k] = out[k] + part_ref[k] if has_part else out[k]


def down_last_kernel(mine, group, *refs):
    count = len(group)
    v_refs, (ch_ref, tab_ref, tabt_ref, *rest) = refs[:count], refs[count:]
    nodes, (part_ref, g_ref, *scratch) = rest[:NODES], rest[NODES:]
    core, y = lax.axis_index("c"), lax.axis_index("y")
    for quad in range(2):

        @pl.when(core == (quad if mine else 1 - quad))
        def _():
            out = quads_down((quad,), group, v_refs, ch_ref, tab_ref, tabt_ref, nodes, *scratch)
            for i in range(4):
                g_ref[i ^ y] = out[4 * quad + i] + part_ref[4 * quad + i]


def down(kernel, name, sections, group, v, tables, nodes, *part):
    count = len(group)
    args = (*v, *tables[1:], *nodes, *part)
    return pl.pallas_call(
        kernel,
        out_shape=single(sections, M, 2 * L),
        in_specs=[VMEM] * len(args),
        out_specs=VMEM,
        scratch_shapes=[
            pltpu.VMEM((count, 2, L, 2 * L), BF16),
            pltpu.VMEM((2, count, 2, L, 2 * L), BF16),
            pltpu.VMEM((4, 2, count * L, 2 * L), BF16),
        ],
        compiler_params=PARAMS,
        name=name,
    )(*args)


def sum_kernel(own_ref, a_ref, b_ref, c_ref, out_ref):
    total = (own_ref[...] + a_ref[...]) + (b_ref[...] + c_ref[...])
    out_ref[...] = 2.0 * adjoint(padded(total))[:M]


def sum_up(own, a, b, c):
    return pl.pallas_call(
        sum_kernel,
        out_shape=single(M, 2 * L),
        in_specs=[VMEM] * 4,
        out_specs=VMEM,
        compiler_params=PARAMS,
        name="sum_up",
    )(own, a, b, c)


def store_kernel(*refs):
    parts, (out_ref, rows_ref, buffer_ref, sems) = refs[:ND], refs[ND:]
    core, y = lax.axis_index("c"), lax.axis_index("y")
    for i in range(ND):
        place = (4 * core if i < 4 else 4 * (1 - core)) + (y ^ (i % 4))
        at = pl.ds(pl.multiple_of(place * L, L), M)
        rows_ref[0, at, :] = parts[i][:, :L]
        rows_ref[1, at, :] = parts[i][:, L:]
    copies = []
    for i, (a, b) in enumerate(ROWS):
        for m in range(a, b):
            rows = pl.ds(m, ND, stride=L)
            buffer_ref[:, m * W : m * W + M] = rows_ref[0, rows, :][:, :M]
            buffer_ref[:, m * W + M : (m + 1) * W] = rows_ref[1, rows, :][:, :M]
        at = (slice(None), pl.ds(a * W, (b - a) * W))
        copies.append(pltpu.make_async_copy(buffer_ref.at[at], out_ref.at[at], sems.at[i]))
        copies[-1].start()
    for copy in copies:
        copy.wait()


def store(parts):
    return pl.pallas_call(
        store_kernel,
        out_shape=single(ND, M * W),
        in_specs=[VMEM] * ND,
        out_specs=HBM,
        scratch_shapes=[pltpu.VMEM((2, ND * L, L), F32), *ROW_SCRATCH],
        compiler_params=PARAMS,
        name="store",
    )(*parts)


def shards(coupling, propagation, frequency_offset, measured):
    swap = [(0, 1), (1, 0)]

    def exchange(i, x):
        return lax.ppermute(x, ("zl", "x"), [(s, s ^ OFFSETS[i]) for s in range(ND)]) if OFFSETS[i] else x

    def turned(i, x):
        return lax.ppermute(x, "y", [(s, s ^ i) for s in range(4)])

    tables, nodes_first, a_first = up(UP_GROUPS[0], frequency_offset, propagation, coupling)
    nodes_second, a_second = up_second(UP_GROUPS[1], tables)
    nodes, a = (*nodes_first, *nodes_second), (*a_first, *a_second)
    h, r, p, q = half([exchange(i, x) for i, x in enumerate(a)])
    other = lax.ppermute(h, ("zh", "zl"), [(0, 3), (1, 2), (2, 1), (3, 0)])
    v = top(r, pick(measured), p, q, h, other)
    v = [exchange(i, x) for i, x in enumerate(v)]

    one, two = DOWN_GROUPS
    part = down(functools.partial(down_whole_kernel, one, False), "down_1", ND, one, [v[i] for i in one], tables, nodes)
    last = [v[i] for i in two]
    theirs = down(functools.partial(down_last_kernel, False, two), "down_theirs", 4, two, last, tables, nodes, part)
    received = lax.ppermute(theirs, "c", swap)
    mine = down(functools.partial(down_last_kernel, True, two), "down_mine", 4, two, last, tables, nodes, part)

    g = mine + received
    order = (3, 1, 2)
    total = sum_up(g[0], *[turned(i, g[i]) for i in order])
    turns = {i: turned(i, total) for i in order}
    parts = [total] + [turns[i] for i in (1, 2, 3)]
    parts += [lax.ppermute(x, "c", swap) for x in parts]
    return store(parts)


def solution(mesh):
    fine = Mesh(mesh.devices.reshape(2, 2, 4, 4, 2), ("zh", "zl", "x", "y", "c"))
    sec, freq = ("zh", "zl", "x"), ("y", "c")
    return jax.shard_map(
        shards,
        mesh=fine,
        in_specs=(P(sec, None), P(sec, None), P(freq), P(freq, None)),
        out_specs=P(sec, None),
        check_vma=False,
    )
```

```python
import functools

import jax
import jax.numpy as jnp
from jax import lax
from jax.experimental import pallas as pl
from jax.experimental.pallas import tpu as pltpu
from jax.sharding import Mesh, PartitionSpec as P

M = 120
W = 2 * M
L = 128
ND = 8
F32, BF16 = jnp.float32, jnp.bfloat16
PARAMS = pltpu.CompilerParams(vmem_limit_bytes=20 * 1024 * 1024)
VMEM = pl.BlockSpec(memory_space=pltpu.VMEM)
SMEM = pl.BlockSpec(memory_space=pltpu.SMEM)
HBM = pl.BlockSpec(memory_space=pltpu.HBM)

OFFSETS = (2, 6, 4, 7, 3, 5, 1, 0)
UP_GROUPS = ((0, 1, 2), (3, 4, 5, 6, 7))
DOWN_GROUPS = ((7,), (0, 1, 2, 3, 4, 5, 6))
NODES = 2 * len(UP_GROUPS)
ROWS = ((0, 32), (32, 64), (64, 96), (96, 120))


def single(*dims):
    return jax.ShapeDtypeStruct(dims, F32)


def halves(*dims):
    return jax.ShapeDtypeStruct((*dims, 2, L, 2 * L), BF16)


def split(x):
    high = x.astype(BF16)
    return high, (x - high.astype(F32)).astype(BF16)


def right_form(x):
    real, imag = x[:, :L], x[:, L:]
    return jnp.concatenate([x, jnp.concatenate([-imag, real], axis=1)], axis=0)


def product(left, right):
    (left_high, left_low), (right_high, right_low) = left, right
    right_high, right_low = right_form(right_high), right_form(right_low)
    return jnp.dot(
        jnp.concatenate([left_high, left_low, left_high], axis=1),
        jnp.concatenate([right_high, right_high, right_low], axis=0),
        preferred_element_type=F32,
    )


def load(ref, *at):
    return ref[(*at, 0)], ref[(*at, 1)]


def keep(ref, x, *at):
    ref[(*at, 0)], ref[(*at, 1)] = split(x)


def scaled(x, cosine, sine):
    real, imag = x[:, :L], x[:, L:]
    return jnp.concatenate([cosine * real - sine * imag, cosine * imag + sine * real], axis=1)


def adjoint(x):
    return jnp.concatenate([x[:, :L].T, -x[:, L:].T], axis=1)


def padded(x):
    return jnp.concatenate([x, jnp.zeros((L - M, 2 * L), F32)], axis=0)


def start_rows(flat_ref, buffer_ref, sems):
    copies = []
    for i, (a, b) in enumerate(ROWS):
        at = (slice(None), pl.ds(a * W, (b - a) * W))
        copies.append(pltpu.make_async_copy(flat_ref.at[at], buffer_ref.at[at], sems.at[i]))
        copies[-1].start()
    return copies


def unpack_rows(copies, buffer_ref, out_ref):
    zeros = jnp.zeros((ND, L - M), F32)
    for (a, b), copy in zip(ROWS, copies):
        copy.wait()
        for part in range(2):
            for start in range(a, b, ND):
                firsts = [m * W + part * M for m in range(start, start + ND)]
                rows = [jnp.concatenate([buffer_ref[:, i : i + M], zeros], axis=1) for i in firsts]
                block = jnp.swapaxes(jnp.stack(rows), 0, 1)
                for k in range(ND):
                    out_ref[part, k * L + start : k * L + start + ND, :] = block[k]
    for k in range(ND):
        out_ref[:, k * L + M : (k + 1) * L, :] = jnp.zeros((2, L - M, L), F32)


def unpacked(rows_ref, start):
    return jnp.concatenate([rows_ref[0, pl.ds(start, L), :], rows_ref[1, pl.ds(start, L), :]], axis=1)


ROW_SCRATCH = [pltpu.VMEM((ND, M * W), F32), pltpu.SemaphoreType.DMA((len(ROWS),))]


def number():
    return lax.axis_index("zl") * 4 + lax.axis_index("x")


def owned():
    return number() ^ (lax.axis_index("zh") * 4)


def scalings(tab_ref, tabt_ref):
    def columns(x, k, f):
        i = f * ND + k
        return scaled(x, tab_ref[0, i : i + 1, :], tab_ref[1, i : i + 1, :])

    def rows(x, k, f):
        i = f * ND + k
        return scaled(x, tabt_ref[0, :, i : i + 1], tabt_ref[1, :, i : i + 1])

    return columns, rows


def up_group(group, a_refs, c_ref, ch_ref, tab_ref, tabt_ref, p_ref, q_ref, lhs_ref):
    columns, rows = scalings(tab_ref, tabt_ref)
    count = len(group)
    for j in range(4):
        low, up = 2 * j, 2 * j + 1
        c_up = unpacked(c_ref, up * L)
        for i, f in enumerate(group):
            at = slice(i * L, (i + 1) * L)
            lhs_ref[j, 0, at], lhs_ref[j, 1, at] = split(columns(c_up, low, f))
        res = product(load(lhs_ref, j), load(ch_ref, low))
        for i, f in enumerate(group):
            one = res[i * L : (i + 1) * L]
            keep(p_ref, rows(one, up, f) if j % 2 == 0 else one, j, i)
    for i, f in enumerate(group):
        keep(q_ref, rows(product(load(p_ref, 1, i), load(p_ref, 0, i)), 3, f), 0, i)
    for i, f in enumerate(group):
        keep(q_ref, product(load(p_ref, 3, i), load(p_ref, 2, i)), 1, i)
    for i, f in enumerate(group):
        a_refs[i][...] = rows(product(load(q_ref, 1, i), load(q_ref, 0, i)), 7, f)[:M]


def up_kernel(group, freq_hbm, prop_hbm, flat_hbm, c_ref, ch_ref, tab_ref, tabt_ref, p_ref, q_ref, *refs):
    count = len(group)
    a_refs, (lhs_ref, freq_ref, prop_ref, small, buffer_ref, sems) = refs[:count], refs[count:]
    first = pltpu.make_async_copy(freq_hbm, freq_ref, small.at[0])
    second = pltpu.make_async_copy(prop_hbm, prop_ref, small.at[1])
    first.start()
    second.start()
    copies = start_rows(flat_hbm, buffer_ref, sems)
    tab_ref[...] = jnp.zeros(tab_ref.shape, F32)
    first.wait()
    second.wait()
    for f in range(ND):
        phase = prop_ref[...] * freq_ref[owned() ^ OFFSETS[f]]
        tab_ref[0, f * ND : (f + 1) * ND, 0:M] = jnp.cos(phase)
        tab_ref[1, f * ND : (f + 1) * ND, 0:M] = jnp.sin(phase)
    tabt_ref[0] = tab_ref[0].T
    tabt_ref[1] = tab_ref[1].T
    unpack_rows(copies, buffer_ref, c_ref)
    for k in range(ND):
        keep(ch_ref, unpacked(c_ref, k * L), k)
    up_group(group, a_refs, c_ref, ch_ref, tab_ref, tabt_ref, p_ref, q_ref, lhs_ref)


def up_second_kernel(group, c_ref, ch_ref, tab_ref, tabt_ref, p_ref, q_ref, *refs):
    a_refs, (lhs_ref,) = refs[: len(group)], refs[len(group) :]
    up_group(group, a_refs, c_ref, ch_ref, tab_ref, tabt_ref, p_ref, q_ref, lhs_ref)


def up_outs(group):
    count = len(group)
    return (halves(4, count), halves(2, count)) + (single(M, 2 * L),) * count


def lhs_scratch(group):
    return pltpu.VMEM((4, 2, len(group) * L, 2 * L), BF16)


def in_hbm(x):
    return pltpu.with_memory_space_constraint(x, pltpu.HBM)


def up(group, freq, prop, flat):
    tables = (single(2, ND * L, L), halves(ND), single(2, ND * ND, L), single(2, L, ND * ND))
    outs = tables + up_outs(group)
    res = pl.pallas_call(
        functools.partial(up_kernel, group),
        out_shape=outs,
        in_specs=[HBM, HBM, HBM],
        out_specs=(VMEM,) * len(outs),
        scratch_shapes=[
            lhs_scratch(group),
            pltpu.SMEM((ND,), F32),
            pltpu.VMEM((ND, M), F32),
            pltpu.SemaphoreType.DMA((2,)),
            *ROW_SCRATCH,
        ],
        compiler_params=PARAMS,
        name="up",
    )(in_hbm(freq), in_hbm(prop), in_hbm(flat))
    return res[:4], res[4:6], res[6:]


def up_second(group, tables):
    outs = up_outs(group)
    res = pl.pallas_call(
        functools.partial(up_second_kernel, group),
        out_shape=outs,
        in_specs=[VMEM] * 4,
        out_specs=(VMEM,) * len(outs),
        scratch_shapes=[lhs_scratch(group)],
        compiler_params=PARAMS,
        name="up_second",
    )(*tables)
    return res[:2], res[2:]


def half_kernel(*refs):
    received, (h_ref, r_ref, p_ref, q_ref) = refs[:ND], refs[ND:]
    me = number()
    for i, offset in enumerate(OFFSETS):
        keep(r_ref, padded(received[i][...]), me ^ offset)
    for j in range(4):
        keep(p_ref, product(load(r_ref, 2 * j + 1), load(r_ref, 2 * j)), j)
    for j in range(2):
        keep(q_ref, product(load(p_ref, 2 * j + 1), load(p_ref, 2 * j)), j)
    h_ref[...] = product(load(q_ref, 1), load(q_ref, 0))[:M]


def half(received):
    return pl.pallas_call(
        half_kernel,
        out_shape=(single(M, 2 * L), halves(ND), halves(4), halves(2)),
        in_specs=[VMEM] * ND,
        out_specs=(VMEM,) * 4,
        compiler_params=PARAMS,
        name="half",
    )(*received)


def pick_kernel(flat_ref, m_ref, rows_ref, buffer_ref, sems):
    unpack_rows(start_rows(flat_ref, buffer_ref, sems), buffer_ref, rows_ref)
    m_ref[...] = unpacked(rows_ref, pl.multiple_of(owned() * L, L))


def pick(flat):
    return pl.pallas_call(
        pick_kernel,
        out_shape=single(L, 2 * L),
        in_specs=[HBM],
        out_specs=VMEM,
        scratch_shapes=[pltpu.VMEM((2, ND * L, L), F32), *ROW_SCRATCH],
        compiler_params=PARAMS,
        name="pick",
    )(in_hbm(flat))


def top_kernel(r_ref, m_ref, p_ref, q_ref, h_ref, other_ref, *refs):
    v_refs, leaf_ref = refs[:ND], refs[ND]
    upper = lax.axis_index("zh") == 1
    own, other = padded(h_ref[...]), padded(other_ref[...])
    h0 = split(jnp.where(upper, other, own))
    h1 = split(jnp.where(upper, own, other))
    misfit = split(adjoint(product(h1, h0) - m_ref[...]))
    left = [jnp.where(upper, a, b) for a, b in zip(h0, misfit)]
    right = [jnp.where(upper, a, b) for a, b in zip(misfit, h1)]
    v = split(product(left, right))
    v0, v1 = split(product(v, load(q_ref, 1))), split(product(load(q_ref, 0), v))
    pairs = (
        product(v0, load(p_ref, 1)),
        product(load(p_ref, 0), v0),
        product(v1, load(p_ref, 3)),
        product(load(p_ref, 2), v1),
    )
    for j in range(4):
        pair = split(pairs[j])
        leaf_ref[2 * j] = product(pair, load(r_ref, 2 * j + 1))[:M]
        leaf_ref[2 * j + 1] = product(load(r_ref, 2 * j), pair)[:M]
    me = number()
    for i, offset in enumerate(OFFSETS):
        v_refs[i][...] = leaf_ref[me ^ offset]


def top(r, m, p, q, h, other):
    return pl.pallas_call(
        top_kernel,
        out_shape=(single(M, 2 * L),) * ND,
        in_specs=[VMEM] * 6,
        out_specs=(VMEM,) * ND,
        scratch_shapes=[pltpu.VMEM((ND, M, 2 * L), F32)],
        compiler_params=PARAMS,
        name="top",
    )(r, m, p, q, h, other)


def quads_down(quads, group, v_refs, ch_ref, tab_ref, tabt_ref, nodes, v_ref, vq_ref, vp_ref):
    columns, rows = scalings(tab_ref, tabt_ref)
    count = len(group)
    place = {f: (n, i) for n, fs in enumerate(UP_GROUPS) for i, f in enumerate(fs)}

    def node(level, j, f):
        n, i = place[f]
        return load(nodes[2 * n + level], j, i)

    for i, f in enumerate(group):
        keep(v_ref, columns(padded(v_refs[i][...]), 7, f), i)
    for quad in quads:
        for i, f in enumerate(group):
            v = load(v_ref, i)
            if quad == 0:
                keep(vq_ref, columns(product(v, node(1, 1, f)), 3, f), 0, i)
            else:
                keep(vq_ref, product(node(1, 0, f), v), 1, i)
    for quad in quads:
        for i, f in enumerate(group):
            v = load(vq_ref, quad, i)
            at = slice(i * L, (i + 1) * L)
            res = columns(product(v, node(0, 2 * quad + 1, f)), 4 * quad + 1, f)
            vp_ref[2 * quad, 0, at], vp_ref[2 * quad, 1, at] = split(res)
            res = product(node(0, 2 * quad, f), v)
            vp_ref[2 * quad + 1, 0, at], vp_ref[2 * quad + 1, 1, at] = split(res)
    out = {}
    for quad in quads:
        for j in (2 * quad, 2 * quad + 1):
            low, up = 2 * j, 2 * j + 1
            res = product(load(vp_ref, j), load(ch_ref, up))
            g_low = g_up = None
            for i, f in enumerate(group):
                at = slice(i * L, (i + 1) * L)
                one = columns(res[at], low, f)
                g_low = one if i == 0 else g_low + one
                one = rows(product(load(ch_ref, low), (vp_ref[j, 0, at], vp_ref[j, 1, at])), low, f)
                g_up = one if i == 0 else g_up + one
            out[low], out[up] = g_low[:M], g_up[:M]
    return out


def down_whole_kernel(group, has_part, *refs):
    count = len(group)
    v_refs, (ch_ref, tab_ref, tabt_ref, *rest) = refs[:count], refs[count:]
    nodes, rest = rest[:NODES], rest[NODES:]
    part_ref = rest.pop(0) if has_part else None
    g_ref, *scratch = rest
    out = quads_down((0, 1), group, v_refs, ch_ref, tab_ref, tabt_ref, nodes, *scratch)
    for k in range(ND):
        g_ref[k] = out[k] + part_ref[k] if has_part else out[k]


def down_last_kernel(mine, group, *refs):
    count = len(group)
    v_refs, (ch_ref, tab_ref, tabt_ref, *rest) = refs[:count], refs[count:]
    nodes, (part_ref, g_ref, *scratch) = rest[:NODES], rest[NODES:]
    core, y = lax.axis_index("c"), lax.axis_index("y")
    for quad in range(2):

        @pl.when(core == (quad if mine else 1 - quad))
        def _():
            out = quads_down((quad,), group, v_refs, ch_ref, tab_ref, tabt_ref, nodes, *scratch)
            for i in range(4):
                g_ref[i ^ y] = out[4 * quad + i] + part_ref[4 * quad + i]


def down(kernel, name, sections, group, v, tables, nodes, *part):
    count = len(group)
    args = (*v, *tables[1:], *nodes, *part)
    return pl.pallas_call(
        kernel,
        out_shape=single(sections, M, 2 * L),
        in_specs=[VMEM] * len(args),
        out_specs=VMEM,
        scratch_shapes=[
            pltpu.VMEM((count, 2, L, 2 * L), BF16),
            pltpu.VMEM((2, count, 2, L, 2 * L), BF16),
            pltpu.VMEM((4, 2, count * L, 2 * L), BF16),
        ],
        compiler_params=PARAMS,
        name=name,
    )(*args)


def sum_kernel(own_ref, a_ref, b_ref, c_ref, out_ref):
    total = (own_ref[...] + a_ref[...]) + (b_ref[...] + c_ref[...])
    out_ref[...] = 2.0 * adjoint(padded(total))[:M]


def sum_up(own, a, b, c):
    return pl.pallas_call(
        sum_kernel,
        out_shape=single(M, 2 * L),
        in_specs=[VMEM] * 4,
        out_specs=VMEM,
        compiler_params=PARAMS,
        name="sum_up",
    )(own, a, b, c)


def store_kernel(*refs):
    parts, (out_ref, rows_ref, buffer_ref, sems) = refs[:ND], refs[ND:]
    core, y = lax.axis_index("c"), lax.axis_index("y")
    for i in range(ND):
        place = (4 * core if i < 4 else 4 * (1 - core)) + (y ^ (i % 4))
        at = pl.ds(pl.multiple_of(place * L, L), M)
        rows_ref[0, at, :] = parts[i][:, :L]
        rows_ref[1, at, :] = parts[i][:, L:]
    copies = []
    for i, (a, b) in enumerate(ROWS):
        for m in range(a, b):
            rows = pl.ds(m, ND, stride=L)
            buffer_ref[:, m * W : m * W + M] = rows_ref[0, rows, :][:, :M]
            buffer_ref[:, m * W + M : (m + 1) * W] = rows_ref[1, rows, :][:, :M]
        at = (slice(None), pl.ds(a * W, (b - a) * W))
        copies.append(pltpu.make_async_copy(buffer_ref.at[at], out_ref.at[at], sems.at[i]))
        copies[-1].start()
    for copy in copies:
        copy.wait()


def store(parts):
    return pl.pallas_call(
        store_kernel,
        out_shape=single(ND, M * W),
        in_specs=[VMEM] * ND,
        out_specs=HBM,
        scratch_shapes=[pltpu.VMEM((2, ND * L, L), F32), *ROW_SCRATCH],
        compiler_params=PARAMS,
        name="store",
    )(*parts)


def shards(coupling, propagation, frequency_offset, measured):
    swap = [(0, 1), (1, 0)]

    def exchange(i, x):
        return lax.ppermute(x, ("zl", "x"), [(s, s ^ OFFSETS[i]) for s in range(ND)]) if OFFSETS[i] else x

    def turned(i, x):
        return lax.ppermute(x, "y", [(s, s ^ i) for s in range(4)])

    tables, nodes_first, a_first = up(UP_GROUPS[0], frequency_offset, propagation, coupling)
    nodes_second, a_second = up_second(UP_GROUPS[1], tables)
    nodes, a = (*nodes_first, *nodes_second), (*a_first, *a_second)
    h, r, p, q = half([exchange(i, x) for i, x in enumerate(a)])
    other = lax.ppermute(h, ("zh", "zl"), [(0, 3), (1, 2), (2, 1), (3, 0)])
    v = top(r, pick(measured), p, q, h, other)
    v = [exchange(i, x) for i, x in enumerate(v)]

    one, two = DOWN_GROUPS
    part = down(functools.partial(down_whole_kernel, one, False), "down_1", ND, one, [v[i] for i in one], tables, nodes)
    last = [v[i] for i in two]
    theirs = down(functools.partial(down_last_kernel, False, two), "down_theirs", 4, two, last, tables, nodes, part)
    received = lax.ppermute(theirs, "c", swap)
    mine = down(functools.partial(down_last_kernel, True, two), "down_mine", 4, two, last, tables, nodes, part)

    g = mine + received
    order = (3, 1, 2)
    total = sum_up(g[0], *[turned(i, g[i]) for i in order])
    turns = {i: turned(i, total) for i in order}
    parts = [total] + [turns[i] for i in (1, 2, 3)]
    parts += [lax.ppermute(x, "c", swap) for x in parts]
    return store(parts)


def solution(mesh):
    fine = Mesh(mesh.devices.reshape(2, 2, 4, 4, 2), ("zh", "zl", "x", "y", "c"))
    sec, freq = ("zh", "zl", "x"), ("y", "c")
    return jax.shard_map(
        shards,
        mesh=fine,
        in_specs=(P(sec, None), P(sec, None), P(freq), P(freq, None)),
        out_specs=P(sec, None),
        check_vma=False,
    )
```
